32 devices in a mesh: orb: 2 (over y), aux: 16 (over z, x, core).
Axes of the slice: x: 2, y: 2, z: 4, core: 2. Of those that a mesh axis runs over, the one named last changes fastest.
Arguments:
- factors: bfloat16 [4, 32768, 512], P('orb', 'aux'), may hold values from -0.5 to 0.5
- occ_energy: float32 [4], replicated, may hold values from -2 to -0.5
- virt_energy: float32 [4, 512], replicated, may hold values from 0.2 to 3
- tile_table: int32 [4, 3], replicated, may hold values from 0 to 3, as said below
Outputs:
- gamma: bfloat16 [4, 32768, 512], P('orb', 'aux')
The draws below stay inside these ranges and needn't reach their ends.
Inputs may be any that keep to these rules, and one draw needn't show every extreme that they name: Row t names two different blocks and the group tile_table[t, 2] that computes the tile. Each group computes at most 4 tiles, and some group exactly 4. Of the blocks owned by another group, the tiles of one group name at most one.
All inputs are finite; a program needn't handle non-finite values.
Results may differ from the reference program's by a relative error of at most 0.0053.
Values may be sent and summed in bfloat16 or wider, within the bound.
No kernel may reach another device: no remote copies, remote signals or barrier semaphores. Data moves between devices by JAX's collectives and lax.ppermute only.
A program may use at most 192 MiB of HBM per device.

```python
import math
import jax
import jax.numpy as jnp
from jax import lax

VB = 512
NAUX = 32768
BLK_GRP = 2
TPG = 2
NB = 4
TILES = 4
N_ORB = 2


def draw_tile_table(key, part):
    groups = N_ORB
    owned = BLK_GRP
    keys = jax.random.split(jax.random.fold_in(key, 7), 6)
    order = jax.random.permutation(keys[0], groups)
    offsets = jax.random.randint(keys[1], (groups // 2,), 0, TPG + 1).at[0].set(TPG)
    counts = jnp.zeros((groups,), jnp.int32).at[order[0::2]].set(TPG + offsets).at[order[1::2]].set(TPG - offsets)
    limits = jnp.cumsum(counts)
    slots = jnp.arange(TILES, dtype=jnp.int32)
    sorted_helper = jnp.sum((slots[:, None] >= limits[None, :]).astype(jnp.int32), axis=1)
    helper = sorted_helper[jax.random.permutation(keys[2], TILES)]
    chosen = jax.random.randint(keys[3], (groups, groups), 0, owned)
    own_blocks = helper[:, None] * owned + jnp.arange(owned, dtype=jnp.int32)[None, :]
    other_blocks = jnp.arange(groups, dtype=jnp.int32)[None, :] * owned + chosen[helper]
    listing = jnp.concatenate([own_blocks, other_blocks], axis=1)
    count = owned + groups - 1
    first_raw = jax.random.randint(keys[4], (TILES,), 0, count)
    second_raw = (first_raw + 1 + jax.random.randint(keys[5], (TILES,), 0, count - 1)) % count
    first_pos = jnp.where(first_raw < owned + helper, first_raw, first_raw + 1)
    second_pos = jnp.where(second_raw < owned + helper, second_raw, second_raw + 1)
    first = jnp.take_along_axis(listing, first_pos[:, None], axis=1)[:, 0]
    second = jnp.take_along_axis(listing, second_pos[:, None], axis=1)[:, 0]
    return jnp.stack([first, second, helper], axis=1).astype(jnp.int32)


def block_scale(rng, extent, shards, least, top_value):
    level, own = 1.0, jax.random.fold_in(rng, 6)
    for position, shards_of in shards:
        heights = jnp.exp(jax.random.uniform(jax.random.fold_in(own, position), (shards_of,), jnp.float32, least / len(shards), top_value / len(shards)))
        level = level * jnp.repeat(heights, extent[position] // shards_of).reshape([-1 if axis == position else 1 for axis in range(len(extent))])
    return level


def noise(own_key, dims, spread, limit, cuts=(), kind=jnp.bfloat16):
    values = spread * jax.random.normal(own_key, dims, jnp.float32)
    if cuts:
        values = values * block_scale(own_key, dims, cuts, -0.22, 0.18)
    return jnp.clip(values, -limit, limit).astype(kind)


def setup_inputs(seed: int = 0) -> dict:
    key_of = jax.random.split(jax.random.key(seed), 5)
    factors = noise(key_of[0], (NB, NAUX, VB), 0.08, 0.5, ((0, 2), (1, 16)))
    occ_energy = jnp.clip(jax.random.uniform(key_of[1], (NB,), jnp.float32, -2.0, -0.5), -2.0, -0.5)
    virt_energy = jnp.clip(jnp.exp(jax.random.uniform(key_of[2], (NB, VB), jnp.float32, math.log(0.2), math.log(3.0))), 0.2, 3.0)
    tile_table = draw_tile_table(jax.random.fold_in(key_of[4], 71), 0)
    return dict(factors=factors, occ_energy=occ_energy, virt_energy=virt_energy, tile_table=tile_table)


def reference(factors, occ_energy, virt_energy, tile_table):
    def tile_amp(index):
        first = tile_table[index, 0]
        second = tile_table[index, 1]
        block_p = lax.dynamic_index_in_dim(factors, first, 0, keepdims=False)
        block_q = lax.dynamic_index_in_dim(factors, second, 0, keepdims=False)
        products = lax.dot_general(block_p, block_q, (((0,), (0,)), ((), ())), preferred_element_type=jnp.float32)
        energy_p = lax.dynamic_index_in_dim(virt_energy, first, 0, keepdims=False)
        energy_q = lax.dynamic_index_in_dim(virt_energy, second, 0, keepdims=False)
        denominators = energy_p[:, None] + energy_q[None, :] - occ_energy[first] - occ_energy[second]
        return (products / denominators).astype(jnp.bfloat16)

    amps = lax.map(tile_amp, jnp.arange(TILES, dtype=jnp.int32))

    def one_block(block):
        owner = block // BLK_GRP

        def add_tile(index, acc):
            first = tile_table[index, 0]
            second = tile_table[index, 1]
            helper = tile_table[index, 2]
            amplitudes = lax.dynamic_index_in_dim(amps, index, 0, keepdims=False)

            def contrib(unused):
                block_p = lax.dynamic_index_in_dim(factors, first, 0, keepdims=False)
                block_q = lax.dynamic_index_in_dim(factors, second, 0, keepdims=False)
                to_first = lax.dot_general(block_q, amplitudes, (((1,), (1,)), ((), ())), preferred_element_type=jnp.float32)
                to_second = jnp.dot(block_p, amplitudes, preferred_element_type=jnp.float32)
                zero = jnp.zeros(to_first.shape, jnp.float32)
                return jnp.where(first == block, to_first, zero) + jnp.where(second == block, to_second, zero)

            def nothing(unused):
                return jnp.zeros((NAUX, VB), jnp.float32)

            touches = jnp.logical_or(first == block, second == block)
            term = lax.cond(touches, contrib, nothing, 0)
            return acc.at[helper].add(term)

        acc = lax.fori_loop(0, TILES, add_tile, jnp.zeros((N_ORB, NAUX, VB), jnp.float32))
        rounded = lax.optimization_barrier(acc.astype(jnp.bfloat16)).astype(jnp.float32)
        is_owner = (jnp.arange(N_ORB, dtype=jnp.int32) == owner)[:, None, None]
        total = jnp.sum(jnp.where(is_owner, acc, rounded), axis=0)
        return total.astype(jnp.bfloat16)

    return lax.map(one_block, jnp.arange(NB, dtype=jnp.int32))
```

```python
import jax
import jax.numpy as jnp
from jax import lax
from jax.sharding import PartitionSpec as P

CAP = 4
WIRE = jnp.bfloat16


def general(factors, occ_energy, virt_energy, tile_table):
    owned = factors.shape[0]
    width = factors.shape[2]
    tiles = tile_table.shape[0]
    groups = lax.axis_size("orb")
    mine = lax.axis_index("orb")
    first = tile_table[:, 0]
    second = tile_table[:, 1]
    helper = tile_table[:, 2]
    block_ids = jnp.arange(owned * groups, dtype=jnp.int32)
    group_ids = jnp.arange(groups, dtype=jnp.int32)
    local_ids = jnp.arange(owned, dtype=jnp.int32)
    touched = (
        (first[:, None] == block_ids[None, :]) | (second[:, None] == block_ids[None, :])
    ).astype(jnp.int32)
    helped = (helper[:, None] == group_ids[None, :]).astype(jnp.int32)
    usage = jnp.sum(helped[:, :, None] * touched[:, None, :], axis=0) > 0
    usage = usage.reshape(groups, groups, owned).astype(jnp.int32)
    own_usage = jnp.take(usage, mine, axis=1)
    send_pick = jnp.sum(own_usage * local_ids[None, :], axis=1)
    outgoing = jnp.take(factors, send_pick, axis=0)
    incoming = lax.all_to_all(outgoing, "orb", split_axis=0, concat_axis=0, tiled=True)
    store = jnp.concatenate([factors, incoming], axis=0)

    def position(block):
        owner = block // owned
        return jnp.where(owner == mine, block % owned, owned + owner)

    is_mine = (helper == mine).astype(jnp.int32)
    tile_ids = jnp.arange(tiles, dtype=jnp.int32)
    earlier = (tile_ids[None, :] < tile_ids[:, None]).astype(jnp.int32)
    rank = jnp.sum(earlier * is_mine[None, :], axis=1)
    slot_ids = jnp.arange(CAP, dtype=jnp.int32)
    picked = is_mine[None, :] * (rank[None, :] == slot_ids[:, None]).astype(jnp.int32)
    valid = jnp.sum(picked, axis=1)
    tile_p = jnp.sum(picked * first[None, :], axis=1)
    tile_q = jnp.sum(picked * second[None, :], axis=1)
    place_p = position(tile_p)
    place_q = position(tile_q)
    energy_p = jnp.take(virt_energy, tile_p, axis=0)
    energy_q = jnp.take(virt_energy, tile_q, axis=0)
    occ_sum = jnp.take(occ_energy, tile_p) + jnp.take(occ_energy, tile_q)
    denominators = energy_p[:, :, None] + energy_q[:, None, :] - occ_sum[:, None, None]

    def partners(slot):
        block_p = lax.dynamic_index_in_dim(store, place_p[slot], 0, keepdims=False)
        block_q = lax.dynamic_index_in_dim(store, place_q[slot], 0, keepdims=False)
        return (block_p, block_q)

    def fill(slot, buffer):
        block_p, block_q = partners(slot)
        return lax.dynamic_update_index_in_dim(buffer, outer(block_p, block_q), slot, 0)

    buffer = lax.fori_loop(0, CAP, fill, jnp.zeros((CAP, width, width), jnp.float32))
    summed = lax.psum(buffer, "aux")
    all_amps = (summed / denominators).astype(jnp.bfloat16)

    def apply_all(slot, gathered):
        block_p, block_q = partners(slot)
        amplitudes = lax.dynamic_index_in_dim(all_amps, slot, 0, keepdims=False)
        amplitudes = jnp.where(valid[slot] > 0, amplitudes, jnp.zeros_like(amplitudes))
        gathered = gathered.at[place_p[slot]].add(right_t(block_q, amplitudes))
        return gathered.at[place_q[slot]].add(right(block_p, amplitudes))

    gathered = lax.fori_loop(0, CAP, apply_all, jnp.zeros(store.shape, jnp.float32))
    helper_part = gathered[owned:].astype(jnp.bfloat16)
    returned = lax.all_to_all(helper_part, "orb", split_axis=0, concat_axis=0, tiled=True)
    landing = (send_pick[:, None] == local_ids[None, :]).astype(jnp.float32)
    gamma = gathered[:owned] + jnp.einsum(
        "dj,dav->jav", landing, returned.astype(jnp.float32), precision=lax.Precision.HIGHEST
    )
    return gamma.astype(jnp.bfloat16)


def outer(a, b):
    return lax.dot_general(a, b, (((0,), (0,)), ((), ())), preferred_element_type=jnp.float32)


def right(a, m):
    return jnp.dot(a, m, preferred_element_type=jnp.float32)


def right_t(a, m):
    return lax.dot_general(a, m, (((1,), (1,)), ((), ())), preferred_element_type=jnp.float32)


def swap(value, axis, bit):
    size = lax.axis_size(axis)
    return lax.ppermute(value, axis, [(i, i ^ (1 << bit)) for i in range(size)])


def halve(part, axis, wires):
    me = lax.axis_index(axis)
    for bit, wire in enumerate(wires):
        high = ((me >> bit) & 1) == 1
        half = part.shape[0] // 2
        low_rows, high_rows = part[:half], part[half:]
        sent = jnp.where(high, low_rows, high_rows).astype(wire)
        kept = jnp.where(high, high_rows, low_rows)
        part = kept + swap(sent, axis, bit).astype(jnp.float32)
    return part


def double(part, axis, bits):
    me = lax.axis_index(axis)
    for bit in reversed(range(bits)):
        high = ((me >> bit) & 1) == 1
        other = swap(part, axis, bit)
        part = jnp.concatenate(
            [jnp.where(high, other, part), jnp.where(high, part, other)], axis=0
        )
    return part


def two_groups(factors, occ_energy, virt_energy, tile_table):
    owned, rows, width = factors.shape
    aux = lax.axis_size("aux")
    bits = aux.bit_length() - 1
    mine = lax.axis_index("orb")
    me = lax.axis_index("aux")
    first, second, helper = tile_table[:, 0], tile_table[:, 1], tile_table[0, 2]
    helps = mine == helper
    low = helper * owned
    foreign_low = (1 - helper) * owned
    foreign = foreign_low
    for block in range(1, owned):
        named = jnp.any((first == foreign_low + block) | (second == foreign_low + block))
        foreign = jnp.where(named, foreign_low + block, foreign)
    foreign_local = foreign - foreign_low

    def count(a, b):
        same = ((first == a) & (second == b)) | ((first == b) & (second == a))
        return jnp.sum(same.astype(jnp.float32))

    shard = width // aux
    offset = jnp.int32(0)
    for bit in range(bits):
        offset = offset + ((me >> bit) & 1) * (width >> (bit + 1))

    def amplitudes(summed, a, b):
        virt_a = lax.dynamic_slice(virt_energy, (a, offset), (1, shard))[0]
        virt_b = lax.dynamic_slice(virt_energy, (b, 0), (1, width))[0]
        occ_a = lax.dynamic_index_in_dim(occ_energy, a, 0, keepdims=False)
        occ_b = lax.dynamic_index_in_dim(occ_energy, b, 0, keepdims=False)
        denominators = virt_a[:, None] + virt_b[None, :] - occ_a - occ_b
        return (count(a, b) * summed / denominators).astype(jnp.bfloat16)

    wires = [jnp.float32] + [WIRE] * (bits - 1)
    half, quarter, early = rows // 2, rows // 4, 3 * rows // 16
    b0 = jnp.where(helps, 0, foreign_local)
    b1 = jnp.where(helps, 1, foreign_local)

    def cut(block, start_helper, start_owner, size):
        start = jnp.where(helps, start_helper, start_owner)
        return lax.dynamic_slice(factors, (block, start, 0), (1, size, width))[0]

    got1 = swap(cut(b0, half, 0, half), "orb", 0)
    got2 = swap(cut(b1, half + quarter, half, quarter), "orb", 0)
    own2 = cut(b1, half, half + quarter, quarter)
    got3 = swap(own2, "orb", 0)
    got4 = swap(cut(b0, early, early, half - early), "orb", 0)
    got5 = swap(cut(b1, early, early, half - early), "orb", 0)

    part01 = outer(factors[0], factors[1])
    amp01 = double(amplitudes(halve(part01, "aux", wires), low, low + 1), "aux", bits)

    def both(value):
        return value + swap(value, "orb", 0)

    own1 = cut(b0, 0, half, half)
    part0f = outer(jnp.where(helps, own1, got1), jnp.where(helps, got1, own1))
    amp0f = double(amplitudes(both(halve(part0f, "aux", wires)), low, foreign), "aux", bits)

    part1f = outer(jnp.where(helps, own2, got2), jnp.where(helps, got2, own2))
    part1f = part1f + jnp.where(helps, outer(factors[1, :half], got1), 0.0)
    amp1f = double(amplitudes(both(halve(part1f, "aux", wires)), low + 1, foreign), "aux", bits)

    back = right(factors[0, :early], amp0f) + right(factors[1, :early], amp1f)
    got6 = swap(back.astype(jnp.bfloat16), "orb", 0)

    whole_f = jnp.concatenate([got1, got2, got3], axis=0)
    gamma0 = (right_t(factors[1], amp01) + right_t(whole_f, amp0f)).astype(jnp.bfloat16)
    gamma1 = (right(factors[0], amp01) + right_t(whole_f, amp1f)).astype(jnp.bfloat16)
    rows0 = jnp.concatenate([got4, got1], axis=0)
    rows1 = jnp.concatenate([got5, got3, got2], axis=0)
    later = (right(rows0, amp0f) + right(rows1, amp1f)).astype(jnp.bfloat16)
    gamma_f = jnp.concatenate([got6, later], axis=0)

    def block(local, at_helper):
        at_owner = jnp.where(local == foreign_local, gamma_f, jnp.zeros_like(gamma_f))
        return jnp.where(helps, at_helper, at_owner)

    return jnp.stack([block(0, gamma0), block(1, gamma1)], axis=0)


def shards(factors, occ_energy, virt_energy, tile_table):
    groups = lax.axis_size("orb")
    aux = lax.axis_size("aux")
    simple = groups == 2 and factors.shape[0] == 2 and tile_table.shape[0] <= CAP
    if simple and aux & (aux - 1) == 0 and factors.shape[1] % 256 == 0:
        return two_groups(factors, occ_energy, virt_energy, tile_table)
    return general(factors, occ_energy, virt_energy, tile_table)


def solution(mesh):
    return jax.shard_map(
        shards,
        mesh=mesh,
        in_specs=(P("orb", "aux", None), P(), P(), P()),
        out_specs=P("orb", "aux", None),
        check_vma=False,
    )
```

```python
import functools

import jax
import jax.numpy as jnp
from jax import lax
from jax.experimental import pallas as pl
from jax.experimental.pallas import tpu as pltpu
from jax.sharding import PartitionSpec as P

CAP = 4
WIRE = jnp.bfloat16
HELPS, FOREIGN, PLACE, COUNTS = 0, 1, 2, 3
PARAMS = pltpu.CompilerParams(vmem_limit_bytes=40 * 1024 * 1024)
SMEM_SPEC = pl.BlockSpec(memory_space=pltpu.SMEM)
ANY_SPEC = pl.BlockSpec(memory_space=pl.ANY)


def general(factors, occ_energy, virt_energy, tile_table):
    owned = factors.shape[0]
    width = factors.shape[2]
    tiles = tile_table.shape[0]
    groups = lax.axis_size("orb")
    mine = lax.axis_index("orb")
    first = tile_table[:, 0]
    second = tile_table[:, 1]
    helper = tile_table[:, 2]
    block_ids = jnp.arange(owned * groups, dtype=jnp.int32)
    group_ids = jnp.arange(groups, dtype=jnp.int32)
    local_ids = jnp.arange(owned, dtype=jnp.int32)
    touched = (
        (first[:, None] == block_ids[None, :]) | (second[:, None] == block_ids[None, :])
    ).astype(jnp.int32)
    helped = (helper[:, None] == group_ids[None, :]).astype(jnp.int32)
    usage = jnp.sum(helped[:, :, None] * touched[:, None, :], axis=0) > 0
    usage = usage.reshape(groups, groups, owned).astype(jnp.int32)
    own_usage = jnp.take(usage, mine, axis=1)
    send_pick = jnp.sum(own_usage * local_ids[None, :], axis=1)
    outgoing = jnp.stack(
        [
            lax.dynamic_index_in_dim(factors, send_pick[group], 0, keepdims=False)
            for group in range(groups)
        ]
    )
    incoming = lax.all_to_all(outgoing, "orb", split_axis=0, concat_axis=0, tiled=True)
    store = jnp.concatenate([factors, incoming], axis=0)

    def position(block):
        owner = block // owned
        return jnp.where(owner == mine, block % owned, owned + owner)

    is_mine = (helper == mine).astype(jnp.int32)
    tile_ids = jnp.arange(tiles, dtype=jnp.int32)
    earlier = (tile_ids[None, :] < tile_ids[:, None]).astype(jnp.int32)
    rank = jnp.sum(earlier * is_mine[None, :], axis=1)
    slot_ids = jnp.arange(CAP, dtype=jnp.int32)
    picked = is_mine[None, :] * (rank[None, :] == slot_ids[:, None]).astype(jnp.int32)
    valid = jnp.sum(picked, axis=1)
    tile_p = jnp.sum(picked * first[None, :], axis=1)
    tile_q = jnp.sum(picked * second[None, :], axis=1)
    place_p = position(tile_p)
    place_q = position(tile_q)
    energy_p = jnp.take(virt_energy, tile_p, axis=0)
    energy_q = jnp.take(virt_energy, tile_q, axis=0)
    occ_sum = jnp.take(occ_energy, tile_p) + jnp.take(occ_energy, tile_q)
    denominators = energy_p[:, :, None] + energy_q[:, None, :] - occ_sum[:, None, None]

    def partners(slot):
        block_p = lax.dynamic_index_in_dim(store, place_p[slot], 0, keepdims=False)
        block_q = lax.dynamic_index_in_dim(store, place_q[slot], 0, keepdims=False)
        return (block_p, block_q)

    def fill(slot, buffer):
        block_p, block_q = partners(slot)
        return lax.dynamic_update_index_in_dim(buffer, outer(block_p, block_q), slot, 0)

    buffer = lax.fori_loop(0, CAP, fill, jnp.zeros((CAP, width, width), jnp.float32))
    summed = lax.psum(buffer, "aux")
    all_amps = (summed / denominators).astype(jnp.bfloat16)

    def apply_all(slot, gathered):
        block_p, block_q = partners(slot)
        amplitudes = lax.dynamic_index_in_dim(all_amps, slot, 0, keepdims=False)
        amplitudes = jnp.where(valid[slot] > 0, amplitudes, jnp.zeros_like(amplitudes))
        gathered = gathered.at[place_p[slot]].add(right_t(block_q, amplitudes))
        return gathered.at[place_q[slot]].add(right(block_p, amplitudes))

    gathered = lax.fori_loop(0, CAP, apply_all, jnp.zeros(store.shape, jnp.float32))
    helper_part = gathered[owned:].astype(jnp.bfloat16)
    returned = lax.all_to_all(helper_part, "orb", split_axis=0, concat_axis=0, tiled=True)
    landing = (send_pick[:, None] == local_ids[None, :]).astype(jnp.float32)
    gamma = gathered[:owned] + jnp.einsum(
        "dj,dav->jav", landing, returned.astype(jnp.float32), precision=lax.Precision.HIGHEST
    )
    return gamma.astype(jnp.bfloat16)


def outer(a, b):
    return lax.dot_general(a, b, (((0,), (0,)), ((), ())), preferred_element_type=jnp.float32)


def right(a, m):
    return jnp.dot(a, m, preferred_element_type=jnp.float32)


def right_t(a, m):
    return lax.dot_general(a, m, (((1,), (1,)), ((), ())), preferred_element_type=jnp.float32)


def swap(value, axis, bit):
    size = lax.axis_size(axis)
    return lax.ppermute(value, axis, [(i, i ^ (1 << bit)) for i in range(size)])


def halve(kept, sent, axis, wires):
    me = lax.axis_index(axis)
    part = kept + swap(sent, axis, 0).astype(jnp.float32)
    for bit, wire in list(enumerate(wires))[1:]:
        high = ((me >> bit) & 1) == 1
        half = part.shape[0] // 2
        low_rows, high_rows = part[:half], part[half:]
        sent = jnp.where(high, low_rows, high_rows).astype(wire)
        kept = jnp.where(high, high_rows, low_rows)
        part = kept + swap(sent, axis, bit).astype(jnp.float32)
    return part


def double(part, axis, bits):
    for bit in reversed(range(1, bits)):
        part = jnp.concatenate([part, swap(part, axis, bit)], axis=0)
    return part, swap(part, axis, 0)


def after(value, *others):
    return lax.optimization_barrier((value, *others))[0]


def plan_kernel(tiles, bits, half, table, factors, plan, pay, sem):
    helper = table[0, 2]
    helps = (lax.axis_index("orb") == helper).astype(jnp.int32)
    low, foreign_low = helper * 2, (1 - helper) * 2
    foreign = jnp.int32(0)
    for t in range(tiles):
        named = (table[t, 0] == foreign_low + 1) | (table[t, 1] == foreign_low + 1)
        foreign = foreign | named.astype(jnp.int32)
    block = jnp.where(helps == 1, 0, foreign)
    copy = pltpu.make_async_copy(
        factors.at[block, pl.ds(pl.multiple_of(helps * half, half), half)], pay, sem
    )
    copy.start()
    me = lax.axis_index("aux")
    place = jnp.int32(0)
    for bit in range(bits):
        place = place * 2 + ((me >> bit) & 1)
    plan[HELPS], plan[FOREIGN], plan[PLACE] = helps, foreign, place
    pairs = ((low, low + 1), (low, foreign_low + foreign), (low + 1, foreign_low + foreign))
    for n, (a, b) in enumerate(pairs):
        count = jnp.int32(0)
        for t in range(tiles):
            p, q = table[t, 0], table[t, 1]
            same = ((p == a) & (q == b)) | ((p == b) & (q == a))
            count = count + same.astype(jnp.int32)
        plan[COUNTS + n] = count
    copy.wait()


def pack_kernel(quarter, plan, factors, pay2, pay3, sems):
    helps, foreign = plan[HELPS], plan[FOREIGN]
    b0, b1 = jnp.where(helps == 1, 0, foreign), jnp.where(helps == 1, 1, foreign)
    second = pl.multiple_of((2 + helps) * quarter, quarter)
    third = pl.multiple_of((3 - helps) * quarter, quarter)
    copies = [
        pltpu.make_async_copy(factors.at[b1, pl.ds(second, quarter)], pay2, sems.at[0]),
        pltpu.make_async_copy(
            factors.at[b1, pl.ds(third, quarter)], pay3.at[pl.ds(0, quarter)], sems.at[1]
        ),
        pltpu.make_async_copy(
            factors.at[b0, pl.ds(quarter, quarter)], pay3.at[pl.ds(quarter, quarter)], sems.at[2]
        ),
        pltpu.make_async_copy(
            factors.at[b1, pl.ds(quarter, quarter)], pay3.at[pl.ds(2 * quarter, quarter)], sems.at[3]
        ),
    ]
    for copy in copies:
        copy.start()
    for copy in copies:
        copy.wait()


def split_halves(acc, kept, sent, core):
    half = kept.shape[0]
    kept[...] = acc[pl.ds(pl.multiple_of(core * half, half), half), :]
    sent[...] = acc[pl.ds(pl.multiple_of((1 - core) * half, half), half), :].astype(sent.dtype)


def own_kernel(plan, blocks, kept, sent, acc):
    step = pl.program_id(0)
    term = outer(blocks[0], blocks[1])

    @pl.when(step == 0)
    def _():
        acc[...] = term

    @pl.when(step > 0)
    def _():
        acc[...] += term

    @pl.when(step == pl.num_programs(0) - 1)
    def _():
        split_halves(acc, kept, sent, lax.axis_index("aux") & 1)


def first_kernel(plan, own, got, kept, sent, acc):
    step = pl.program_id(0)

    @pl.when(step == 0)
    def _():
        acc[...] = jnp.zeros_like(acc)

    @pl.when(plan[HELPS] == 1)
    def _():
        acc[...] += outer(own[0], got[...])

    @pl.when(plan[HELPS] == 0)
    def _():
        acc[...] += outer(got[...], own[0])

    @pl.when(step == pl.num_programs(0) - 1)
    def _():
        split_halves(acc, kept, sent, lax.axis_index("aux") & 1)


def second_kernel(plan, own, got1, got2, kept, sent, acc):
    step = pl.program_id(0)
    last = pl.num_programs(0) - 1

    @pl.when(step == 0)
    def _():
        acc[...] = jnp.zeros_like(acc)

    @pl.when((plan[HELPS] == 1) & (step < last))
    def _():
        acc[...] += outer(own[0], got1[...])

    @pl.when((plan[HELPS] == 1) & (step == last))
    def _():
        acc[...] += outer(own[0], got2[...])

    @pl.when((plan[HELPS] == 0) & (step == last))
    def _():
        acc[...] += outer(got2[...], own[0])

    @pl.when(step == last)
    def _():
        split_halves(acc, kept, sent, lax.axis_index("aux") & 1)


def back_kernel(shard, plan, near0, far0, near1, far1, blocks, back, amp0, amp1):
    arrange(shard, plan, near0, far0, 2, 1, amp0)
    arrange(shard, plan, near1, far1, 1, 0, amp1)
    total = right(blocks[0], amp0[...]) + right(blocks[1], amp1[...])
    back[...] = total.astype(back.dtype)


def arrange(shard, plan, near, far, pairs, which, out):
    count = out.shape[0] // shard
    for source, base in ((near, 0), (far, count // 2)):
        for n in range(count // 2):
            row = pl.multiple_of((plan[PLACE] ^ (base + n)) * shard, shard)
            begin = (n * pairs + which) * shard
            out[pl.ds(row, shard), :] = source[begin : begin + shard, :]


def last_kernel(shard, plan, near0, far0, near1, far1, got1, got2, early_a, early_b, blocks, out, own, amp0, amp1):
    seg = pl.program_id(0)
    helps = plan[HELPS] == 1

    @pl.when(seg == 0)
    def _():
        arrange(shard, plan, near0, far0, 2, 0, own)
        arrange(shard, plan, near0, far0, 2, 1, amp0)
        arrange(shard, plan, near1, far1, 1, 0, amp1)

    @pl.when(helps)
    def _():
        foreign = jnp.where(seg < 2, got1[...], jnp.where(seg == 2, got2[...], early_a[...]))
        out[0] = (right_t(blocks[1], own[...]) + right_t(foreign, amp0[...])).astype(out.dtype)
        out[1] = (right(blocks[0], own[...]) + right_t(foreign, amp1[...])).astype(out.dtype)

    @pl.when(jnp.logical_not(helps))
    def _():
        rows0 = jnp.where(seg == 1, early_a[...], got1[...])
        rows1 = jnp.where(seg == 3, got2[...], early_b[...])
        out[...] = jnp.zeros_like(out)
        total = right(rows0, amp0[...]) + right(rows1, amp1[...])
        out[plan[FOREIGN]] = total.astype(out.dtype)


def put_kernel(quarter, plan, back, gamma_in, gamma, sem):
    @pl.when(plan[HELPS] == 0)
    def _():
        copy = pltpu.make_async_copy(back, gamma.at[plan[FOREIGN], pl.ds(0, quarter)], sem)
        copy.start()
        copy.wait()


def two_groups(factors, occ_energy, virt_energy, tile_table):
    owned, rows, width = factors.shape
    aux = lax.axis_size("aux")
    bits = aux.bit_length() - 1
    tiles = tile_table.shape[0]
    half, quarter = rows // 2, rows // 4
    shard = width // aux
    wires = [jnp.float32] + [WIRE] * (bits - 1)
    dtype = factors.dtype

    plan, pay1 = pl.pallas_call(
        functools.partial(plan_kernel, tiles, bits, half),
        out_shape=(
            jax.ShapeDtypeStruct((8,), jnp.int32),
            jax.ShapeDtypeStruct((half, width), dtype),
        ),
        in_specs=[SMEM_SPEC, ANY_SPEC],
        out_specs=(SMEM_SPEC, ANY_SPEC),
        scratch_shapes=[pltpu.SemaphoreType.DMA],
        compiler_params=PARAMS,
    )(tile_table, factors)
    got1 = swap(pay1, "orb", 0)

    pay2, pay3 = pl.pallas_call(
        functools.partial(pack_kernel, quarter),
        out_shape=(
            jax.ShapeDtypeStruct((quarter, width), dtype),
            jax.ShapeDtypeStruct((3 * quarter, width), dtype),
        ),
        in_specs=[SMEM_SPEC, ANY_SPEC],
        out_specs=(ANY_SPEC, ANY_SPEC),
        scratch_shapes=[pltpu.SemaphoreType.DMA((4,))],
        compiler_params=PARAMS,
    )(plan, factors)

    def halves():
        return (
            jax.ShapeDtypeStruct((width // 2, width), jnp.float32),
            jax.ShapeDtypeStruct((width // 2, width), wires[0]),
        )

    def whole(shape):
        return pl.BlockSpec(shape, lambda i, plan: (0,) * len(shape))

    def run(kernel, steps, specs, out_shape, out_specs, scratch, cost):
        return pl.pallas_call(
            kernel,
            out_shape=out_shape,
            grid_spec=pltpu.PrefetchScalarGridSpec(
                num_scalar_prefetch=1,
                grid=(steps,),
                in_specs=specs,
                out_specs=out_specs,
                scratch_shapes=scratch,
            ),
            compiler_params=PARAMS,
            cost_estimate=pl.CostEstimate(
                flops=cost * 2 * quarter * width * width,
                bytes_accessed=cost * 2 * quarter * width * 2,
                transcendentals=0,
            ),
        )

    half_spec = whole((width // 2, width))
    square = pltpu.VMEM((width, width), jnp.float32)
    block = (1, quarter, width)

    kept, sent = run(
        own_kernel, 4, [pl.BlockSpec((2, quarter, width), lambda i, plan: (0, i, 0))],
        halves(), (half_spec, half_spec), [square], 4,
    )(plan, factors)
    sum01 = halve(kept, sent, "aux", wires)

    helper = tile_table[0, 2]
    low, foreign = helper * owned, (1 - helper) * owned + plan[FOREIGN]
    offset = plan[PLACE] * shard

    def weight(n, a, b):
        virt_a = lax.dynamic_slice(virt_energy, (a, offset), (1, shard))[0]
        virt_b = lax.dynamic_slice(virt_energy, (b, 0), (1, width))[0]
        occ_a = lax.dynamic_index_in_dim(occ_energy, a, 0, keepdims=False)
        occ_b = lax.dynamic_index_in_dim(occ_energy, b, 0, keepdims=False)
        denominators = virt_a[:, None] + virt_b[None, :] - occ_a - occ_b
        return plan[COUNTS + n].astype(jnp.float32) / denominators

    weights = (weight(0, low, low + 1), weight(1, low, foreign), weight(2, low + 1, foreign))
    got1, sum01, *weights = lax.optimization_barrier((got1, sum01, *weights))
    got2 = swap(after(pay2, got1), "orb", 0)

    def both(value):
        return value + swap(value, "orb", 0)

    kept, sent = run(
        first_kernel, 2,
        [
            pl.BlockSpec(
                block,
                lambda i, plan: (
                    jnp.where(plan[HELPS] == 1, 0, plan[FOREIGN]),
                    jnp.where(plan[HELPS] == 1, i, 2 + i),
                    0,
                ),
            ),
            pl.BlockSpec((quarter, width), lambda i, plan: (i, 0)),
        ],
        halves(), (half_spec, half_spec), [square], 2,
    )(plan, factors, got1)
    sum0f = both(halve(kept, sent, "aux", wires))
    shards0 = jnp.concatenate(
        [(sum01 * weights[0]).astype(dtype), (sum0f * weights[1]).astype(dtype)], axis=0
    )
    near0, far0 = double(shards0, "aux", bits)

    got3 = swap(after(pay3, got2), "orb", 0)
    kept, sent = run(
        second_kernel, 3,
        [
            pl.BlockSpec(
                block,
                lambda i, plan: (
                    jnp.where(plan[HELPS] == 1, 1, plan[FOREIGN]),
                    jnp.where(plan[HELPS] == 1, i, 3),
                    0,
                ),
            ),
            pl.BlockSpec((quarter, width), lambda i, plan: (jnp.minimum(i, 1), 0)),
            whole((quarter, width)),
        ],
        halves(), (half_spec, half_spec), [square], 3,
    )(plan, factors, got1, got2)
    sum1f = both(halve(kept, sent, "aux", wires))
    near1, far1 = double((sum1f * weights[2]).astype(dtype), "aux", bits)

    amp_specs = [whole(near0.shape), whole(near0.shape), whole(near1.shape), whole(near1.shape)]
    amp = pltpu.VMEM((width, width), dtype)
    back = run(
        functools.partial(back_kernel, shard), 1,
        amp_specs + [pl.BlockSpec((2, quarter, width), lambda i, plan: (0, 0, 0))],
        jax.ShapeDtypeStruct((quarter, width), dtype), whole((quarter, width)), [amp, amp], 2,
    )(plan, near0, far0, near1, far1, factors)
    got4 = swap(back, "orb", 0)

    def at(helper_blocks, owner_blocks):
        def pick(i, table):
            index = jnp.int32(table[-1])
            for n in range(len(table) - 1):
                index = jnp.where(i == n, table[n], index)
            return index

        return pl.BlockSpec(
            (quarter, width),
            lambda i, plan: (
                jnp.where(plan[HELPS] == 1, pick(i, helper_blocks), pick(i, owner_blocks)),
                0,
            ),
        )

    pieces = pl.BlockSpec((2, quarter, width), lambda i, plan: (0, i, 0))
    gamma = run(
        functools.partial(last_kernel, shard), 4,
        amp_specs
        + [
            at((0, 1, 1, 1), (0, 0, 0, 1)),
            whole((quarter, width)),
            at((0, 0, 0, 0), (1, 1, 1, 1)),
            at((0, 0, 0, 0), (2, 2, 0, 0)),
            pieces,
        ],
        jax.ShapeDtypeStruct(factors.shape, dtype), pieces, [amp, amp, amp], 12,
    )(plan, near0, far0, near1, far1, got1, got2, got3, got3, factors)

    return pl.pallas_call(
        functools.partial(put_kernel, quarter),
        out_shape=jax.ShapeDtypeStruct(factors.shape, dtype),
        in_specs=[SMEM_SPEC, ANY_SPEC, ANY_SPEC],
        out_specs=ANY_SPEC,
        scratch_shapes=[pltpu.SemaphoreType.DMA],
        input_output_aliases={2: 0},
        compiler_params=PARAMS,
    )(plan, got4, gamma)


def shards(factors, occ_energy, virt_energy, tile_table):
    groups = lax.axis_size("orb")
    aux = lax.axis_size("aux")
    simple = groups == 2 and factors.shape[0] == 2 and tile_table.shape[0] <= CAP
    width = factors.shape[2]
    whole_shards = aux & (aux - 1) == 0 and width % (32 * aux) == 0
    if simple and whole_shards and factors.shape[1] % 64 == 0:
        return two_groups(factors, occ_energy, virt_energy, tile_table)
    return general(factors, occ_energy, virt_energy, tile_table)


def solution(mesh):
    return jax.shard_map(
        shards,
        mesh=mesh,
        in_specs=(P("orb", "aux", None), P(), P(), P()),
        out_specs=P("orb", "aux", None),
        check_vma=False,
    )
```

```python
import functools

import jax
import jax.numpy as jnp
from jax import lax
from jax.experimental import pallas as pl
from jax.experimental.pallas import tpu as pltpu
from jax.sharding import PartitionSpec as P

CAP = 4
WIRE = jnp.bfloat16
HELPS, FOREIGN, PLACE, COUNTS, LOW, PARTNER = 0, 1, 2, 3, 6, 7
MEBI = 1024 * 1024
SMEM_SPEC = pl.BlockSpec(memory_space=pltpu.SMEM)
HBM_SPEC = pl.BlockSpec(memory_space=pltpu.HBM)
VMEM_SPEC = pl.BlockSpec(memory_space=pltpu.VMEM)


def general(factors, occ_energy, virt_energy, tile_table):
    owned = factors.shape[0]
    width = factors.shape[2]
    tiles = tile_table.shape[0]
    groups = lax.axis_size("orb")
    mine = lax.axis_index("orb")
    first = tile_table[:, 0]
    second = tile_table[:, 1]
    helper = tile_table[:, 2]
    block_ids = jnp.arange(owned * groups, dtype=jnp.int32)
    group_ids = jnp.arange(groups, dtype=jnp.int32)
    local_ids = jnp.arange(owned, dtype=jnp.int32)
    touched = (
        (first[:, None] == block_ids[None, :]) | (second[:, None] == block_ids[None, :])
    ).astype(jnp.int32)
    helped = (helper[:, None] == group_ids[None, :]).astype(jnp.int32)
    usage = jnp.sum(helped[:, :, None] * touched[:, None, :], axis=0) > 0
    usage = usage.reshape(groups, groups, owned).astype(jnp.int32)
    own_usage = jnp.take(usage, mine, axis=1)
    send_pick = jnp.sum(own_usage * local_ids[None, :], axis=1)
    outgoing = jnp.stack(
        [
            lax.dynamic_index_in_dim(factors, send_pick[group], 0, keepdims=False)
            for group in range(groups)
        ]
    )
    incoming = lax.all_to_all(outgoing, "orb", split_axis=0, concat_axis=0, tiled=True)
    store = jnp.concatenate([factors, incoming], axis=0)

    def position(block):
        owner = block // owned
        return jnp.where(owner == mine, block % owned, owned + owner)

    is_mine = (helper == mine).astype(jnp.int32)
    tile_ids = jnp.arange(tiles, dtype=jnp.int32)
    earlier = (tile_ids[None, :] < tile_ids[:, None]).astype(jnp.int32)
    rank = jnp.sum(earlier * is_mine[None, :], axis=1)
    slot_ids = jnp.arange(CAP, dtype=jnp.int32)
    picked = is_mine[None, :] * (rank[None, :] == slot_ids[:, None]).astype(jnp.int32)
    valid = jnp.sum(picked, axis=1)
    tile_p = jnp.sum(picked * first[None, :], axis=1)
    tile_q = jnp.sum(picked * second[None, :], axis=1)
    place_p = position(tile_p)
    place_q = position(tile_q)
    energy_p = jnp.take(virt_energy, tile_p, axis=0)
    energy_q = jnp.take(virt_energy, tile_q, axis=0)
    occ_sum = jnp.take(occ_energy, tile_p) + jnp.take(occ_energy, tile_q)
    denominators = energy_p[:, :, None] + energy_q[:, None, :] - occ_sum[:, None, None]

    def partners(slot):
        block_p = lax.dynamic_index_in_dim(store, place_p[slot], 0, keepdims=False)
        block_q = lax.dynamic_index_in_dim(store, place_q[slot], 0, keepdims=False)
        return (block_p, block_q)

    def fill(slot, buffer):
        block_p, block_q = partners(slot)
        return lax.dynamic_update_index_in_dim(buffer, outer(block_p, block_q), slot, 0)

    buffer = lax.fori_loop(0, CAP, fill, jnp.zeros((CAP, width, width), jnp.float32))
    summed = lax.psum(buffer, "aux")
    all_amps = (summed / denominators).astype(jnp.bfloat16)

    def apply_all(slot, gathered):
        block_p, block_q = partners(slot)
        amplitudes = lax.dynamic_index_in_dim(all_amps, slot, 0, keepdims=False)
        amplitudes = jnp.where(valid[slot] > 0, amplitudes, jnp.zeros_like(amplitudes))
        gathered = gathered.at[place_p[slot]].add(right_t(block_q, amplitudes))
        return gathered.at[place_q[slot]].add(right(block_p, amplitudes))

    gathered = lax.fori_loop(0, CAP, apply_all, jnp.zeros(store.shape, jnp.float32))
    helper_part = gathered[owned:].astype(jnp.bfloat16)
    returned = lax.all_to_all(helper_part, "orb", split_axis=0, concat_axis=0, tiled=True)
    landing = (send_pick[:, None] == local_ids[None, :]).astype(jnp.float32)
    gamma = gathered[:owned] + jnp.einsum(
        "dj,dav->jav", landing, returned.astype(jnp.float32), precision=lax.Precision.HIGHEST
    )
    return gamma.astype(jnp.bfloat16)


def outer(a, b):
    return lax.dot_general(a, b, (((0,), (0,)), ((), ())), preferred_element_type=jnp.float32)


def right(a, m):
    return jnp.dot(a, m, preferred_element_type=jnp.float32)


def right_t(a, m):
    return lax.dot_general(a, m, (((1,), (1,)), ((), ())), preferred_element_type=jnp.float32)


def swap(value, axis, bit):
    size = lax.axis_size(axis)
    return lax.ppermute(value, axis, [(i, i ^ (1 << bit)) for i in range(size)])


def halve(kept, sent, axis, wires):
    me = lax.axis_index(axis)
    part = kept + swap(sent, axis, 0).astype(jnp.float32)
    for bit, wire in list(enumerate(wires))[1:]:
        high = ((me >> bit) & 1) == 1
        half = part.shape[1] // 2
        low_rows, high_rows = part[:, :half], part[:, half:]
        sent = jnp.where(high, low_rows, high_rows).astype(wire)
        kept = jnp.where(high, high_rows, low_rows)
        part = kept + swap(sent, axis, bit).astype(jnp.float32)
    return part


def double(part, axis, bits):
    part = part[None]
    for bit in reversed(range(1, bits)):
        part = jnp.concatenate([part, swap(part, axis, bit)], axis=0)
    return part, swap(part, axis, 0)


def after(value, *others):
    return lax.optimization_barrier((value, *others))[0]


def start_all(copies):
    for copy in copies:
        copy.start()


def wait_all(copies):
    for copy in copies:
        copy.wait()


def rows_at(unit, start, size):
    return pl.ds(pl.multiple_of(start * unit, unit), size * unit)


def plan_kernel(tiles, bits, step, table, factors, plan, pay, sems):
    helper = table[0, 2]
    helps = (lax.axis_index("orb") == helper).astype(jnp.int32)
    low, foreign_low = helper * 2, (1 - helper) * 2
    foreign = jnp.int32(0)
    for t in range(tiles):
        named = (table[t, 0] == foreign_low + 1) | (table[t, 1] == foreign_low + 1)
        foreign = foreign | named.astype(jnp.int32)
    b0, b1 = jnp.where(helps == 1, 0, foreign), jnp.where(helps == 1, 1, foreign)
    copies = [
        pltpu.make_async_copy(
            factors.at[b0, rows_at(step, 2 * helps, 2)], pay.at[pl.ds(0, 2 * step)], sems.at[0]
        ),
        pltpu.make_async_copy(
            factors.at[b1, rows_at(step, 2 + helps, 1)], pay.at[pl.ds(2 * step, step)], sems.at[1]
        ),
    ]
    start_all(copies)
    me = lax.axis_index("aux")
    place = jnp.int32(0)
    for bit in range(bits):
        place = place * 2 + ((me >> bit) & 1)
    plan[HELPS], plan[FOREIGN], plan[PLACE] = helps, foreign, place
    plan[LOW], plan[PARTNER] = low, foreign_low + foreign
    pairs = ((low, low + 1), (low, foreign_low + foreign), (low + 1, foreign_low + foreign))
    for n, (a, b) in enumerate(pairs):
        count = jnp.int32(0)
        for t in range(tiles):
            p, q = table[t, 0], table[t, 1]
            same = ((p == a) & (q == b)) | ((p == b) & (q == a))
            count = count + same.astype(jnp.int32)
        plan[COUNTS + n] = count
    wait_all(copies)


def weigh_kernel(step, plan, occ, virt, factors, own_weight, weights, pay_a, sem):
    helps = plan[HELPS]
    block = jnp.where(helps == 1, 1, plan[FOREIGN])
    copy = pltpu.make_async_copy(factors.at[block, rows_at(step, 3 - helps, 1)], pay_a, sem)
    copy.start()
    low, partner = plan[LOW], plan[PARTNER]
    _, shard, width = own_weight.shape
    row = lax.broadcasted_iota(jnp.int32, (shard, width), 0)
    column = lax.broadcasted_iota(jnp.int32, (shard, width), 1)
    mine = column == row + plan[PLACE] * shard
    pairs = ((low, low + 1, own_weight, 0), (low, partner, weights, 0), (low + 1, partner, weights, 1))
    for n, (a, b, out, slot) in enumerate(pairs):
        virt_a = jnp.sum(jnp.where(mine, virt[pl.ds(a, 1), :], 0.0), axis=1, keepdims=True)
        denominators = virt_a + virt[pl.ds(b, 1), :] - occ[a] - occ[b]
        out[slot] = plan[COUNTS + n].astype(jnp.float32) / denominators
    copy.wait()


def pack_kernel(step, plan, factors, pay_b, sems):
    helps, foreign = plan[HELPS], plan[FOREIGN]
    blocks = (jnp.where(helps == 1, 0, foreign), jnp.where(helps == 1, 1, foreign))
    copies = [
        pltpu.make_async_copy(
            factors.at[block, pl.ds(step, step)], pay_b.at[pl.ds(n * step, step)], sems.at[n]
        )
        for n, block in enumerate(blocks)
    ]
    start_all(copies)
    wait_all(copies)


def split_halves(acc, pair, kept, sent, core):
    half = kept.shape[1]
    kept[pair] = acc[pl.ds(pl.multiple_of(core * half, half), half), :]
    other = acc[pl.ds(pl.multiple_of((1 - core) * half, half), half), :]
    sent[pair] = other.astype(sent.dtype)


def own_kernel(step, plan, factors, kept, sent, rows, acc, sems):
    del plan
    copies = [
        pltpu.make_async_copy(
            factors.at[:, pl.ds(n * step, step)], rows.at[:, pl.ds(n * step, step)], sems.at[n]
        )
        for n in range(4)
    ]
    start_all(copies)
    for n in range(4):
        copies[n].wait()
        term = outer(rows[0, n * step : (n + 1) * step], rows[1, n * step : (n + 1) * step])
        acc[...] = term if n == 0 else acc[...] + term
    split_halves(acc, 0, kept, sent, lax.axis_index("aux") & 1)


def pair_kernel(step, plan, factors, got, kept, sent, rows0, rows1, acc0, acc1, sems):
    helps, foreign = plan[HELPS], plan[FOREIGN]
    b0, b1 = jnp.where(helps == 1, 0, foreign), jnp.where(helps == 1, 1, foreign)
    copies0 = [
        pltpu.make_async_copy(
            factors.at[b0, rows_at(step, jnp.where(helps == 1, n, 2 + n), 1)],
            rows0.at[pl.ds(n * step, step)],
            sems.at[n],
        )
        for n in range(2)
    ]
    copies1 = [
        pltpu.make_async_copy(
            factors.at[b1, rows_at(step, jnp.where(helps == 1, n, 3), 1)],
            rows1.at[pl.ds(n * step, step)],
            sems.at[2 + n],
        )
        for n in range(3)
    ]
    start_all(copies0 + copies1)

    def cut(ref, n):
        return ref[n * step : (n + 1) * step]

    copies0[0].wait()

    @pl.when(helps == 1)
    def _():
        acc0[...] = outer(cut(rows0, 0), cut(got, 0))

    @pl.when(helps == 0)
    def _():
        acc0[...] = outer(cut(got, 0), cut(rows0, 0))

    copies0[1].wait()

    @pl.when(helps == 1)
    def _():
        acc0[...] += outer(cut(rows0, 1), cut(got, 1))

    @pl.when(helps == 0)
    def _():
        acc0[...] += outer(cut(got, 1), cut(rows0, 1))

    wait_all(copies1)

    @pl.when(helps == 1)
    def _():
        acc1[...] = outer(cut(rows1, 0), cut(got, 0)) + outer(cut(rows1, 1), cut(got, 1))
        acc1[...] += outer(cut(rows1, 2), cut(got, 2))

    @pl.when(helps == 0)
    def _():
        acc1[...] = outer(cut(got, 2), cut(rows1, 2))

    core = lax.axis_index("aux") & 1
    split_halves(acc0, 0, kept, sent, core)
    split_halves(acc1, 1, kept, sent, core)


def arrange(plan, near, far, pair, out):
    count, _, shard, _ = near.shape
    for source, base in ((near, 0), (far, count)):
        for n in range(count):
            row = pl.multiple_of((plan[PLACE] ^ (base + n)) * shard, shard)
            out[pl.ds(row, shard), :] = source[n, pair]


def back_kernel(plan, near, far, blocks, back, amp0, amp1):
    arrange(plan, near, far, 0, amp0)
    arrange(plan, near, far, 1, amp1)
    total = right(blocks[0], amp0[...]) + right(blocks[1], amp1[...])
    back[...] = total.astype(back.dtype)


def last_kernel(plan, near01, far01, near, far, x, a, y, blocks, out, own, amp0, amp1):
    seg = pl.program_id(0)
    helps = plan[HELPS] == 1

    @pl.when(seg == 0)
    def _():
        arrange(plan, near01, far01, 0, own)
        arrange(plan, near, far, 0, amp0)
        arrange(plan, near, far, 1, amp1)

    @pl.when(helps)
    def _():
        foreign = jnp.where(seg < 3, x[...], a[...])
        out[0] = (right_t(blocks[1], own[...]) + right_t(foreign, amp0[...])).astype(out.dtype)
        out[1] = (right(blocks[0], own[...]) + right_t(foreign, amp1[...])).astype(out.dtype)

    @pl.when(jnp.logical_not(helps))
    def _():
        out[...] = jnp.zeros_like(out)

    @pl.when(jnp.logical_not(helps) & (seg >= 2))
    def _():
        rows1 = jnp.where(seg < 3, a[...], y[...])
        total = right(x[...], amp0[...]) + right(rows1, amp1[...])
        out[plan[FOREIGN]] = total.astype(out.dtype)


def late_kernel(step, plan, near, far, got, gamma_in, gamma, amp0, amp1, rows, sem):
    @pl.when(plan[HELPS] == 0)
    def _():
        arrange(plan, near, far, 0, amp0)
        arrange(plan, near, far, 1, amp1)
        total = right(got[:step], amp0[...]) + right(got[step:], amp1[...])
        rows[...] = total.astype(rows.dtype)
        copy = pltpu.make_async_copy(rows, gamma.at[plan[FOREIGN], pl.ds(step, step)], sem)
        copy.start()
        copy.wait()


def put_kernel(step, plan, back, gamma_in, gamma, sem):
    @pl.when(plan[HELPS] == 0)
    def _():
        copy = pltpu.make_async_copy(back, gamma.at[plan[FOREIGN], pl.ds(0, step)], sem)
        copy.start()
        copy.wait()


def two_groups(factors, occ_energy, virt_energy, tile_table):
    owned, rows, width = factors.shape
    aux = lax.axis_size("aux")
    bits = aux.bit_length() - 1
    step = rows // 4
    shard = width // aux
    wires = [jnp.float32] + [WIRE] * (bits - 1)
    dtype = factors.dtype
    dma = pltpu.SemaphoreType.DMA

    def array(*shape, dtype=dtype):
        return jax.ShapeDtypeStruct(shape, dtype)

    def call(kernel, out_shape, in_specs, out_specs, scratch, cost=0, mebi=16, **options):
        return pl.pallas_call(
            kernel,
            out_shape=out_shape,
            in_specs=in_specs,
            out_specs=out_specs,
            scratch_shapes=scratch,
            compiler_params=pltpu.CompilerParams(vmem_limit_bytes=mebi * MEBI),
            cost_estimate=pl.CostEstimate(
                flops=cost * 2 * step * width * width,
                bytes_accessed=2 * step * width * 2,
                transcendentals=0,
            ),
            **options,
        )

    plan, pay1 = call(
        functools.partial(plan_kernel, tile_table.shape[0], bits, step),
        (array(8, dtype=jnp.int32), array(3 * step, width)),
        [SMEM_SPEC, HBM_SPEC],
        (SMEM_SPEC, VMEM_SPEC),
        [dma((2,))],
        mebi=61,
    )(tile_table, factors)
    got1 = swap(pay1, "orb", 0)

    def halves(pairs):
        kept = array(pairs, width // 2, width, dtype=jnp.float32)
        return kept, array(pairs, width // 2, width, dtype=wires[0])

    square = pltpu.VMEM((width, width), jnp.float32)

    own_weight, weights, pay_a = call(
        functools.partial(weigh_kernel, step),
        (
            array(1, shard, width, dtype=jnp.float32),
            array(2, shard, width, dtype=jnp.float32),
            array(step, width),
        ),
        [SMEM_SPEC, SMEM_SPEC, VMEM_SPEC, HBM_SPEC],
        (VMEM_SPEC, VMEM_SPEC, VMEM_SPEC),
        [dma],
    )(plan, occ_energy, virt_energy, factors)

    def own_chain():
        kept, sent = call(
            functools.partial(own_kernel, step),
            halves(1),
            [SMEM_SPEC, HBM_SPEC],
            (VMEM_SPEC, VMEM_SPEC),
            [pltpu.VMEM(factors.shape, dtype), square, dma((4,))],
            4,
        )(plan, factors)
        sum01 = halve(kept, sent, "aux", wires)
        return double((sum01 * own_weight).astype(dtype), "aux", bits)

    def no_chain():
        half = jnp.zeros((aux // 2, 1, shard, width), dtype)
        return half, half

    near01, far01 = lax.cond(plan[COUNTS] > 0, own_chain, no_chain)

    got1, near01, far01, weights, pay_a = lax.optimization_barrier(
        (got1, near01, far01, weights, pay_a)
    )
    got_a = swap(pay_a, "orb", 0)

    kept, sent = call(
        functools.partial(pair_kernel, step),
        halves(2),
        [SMEM_SPEC, HBM_SPEC, VMEM_SPEC],
        (VMEM_SPEC, VMEM_SPEC),
        [
            pltpu.VMEM((2 * step, width), dtype),
            pltpu.VMEM((3 * step, width), dtype),
            square,
            square,
            dma((5,)),
        ],
        5,
    )(plan, factors, got1)
    used = plan[COUNTS + 1] + plan[COUNTS + 2] > 0
    sums = lax.cond(
        used,
        lambda: halve(kept, sent, "aux", wires),
        lambda: jnp.zeros((2, shard, width), jnp.float32),
    )
    pay_b = call(
        functools.partial(pack_kernel, step),
        array(2 * step, width),
        [SMEM_SPEC, HBM_SPEC],
        VMEM_SPEC,
        [dma((2,))],
    )(after(plan, kept), factors)
    sums, got_a, pay_b = lax.optimization_barrier((sums, got_a, pay_b))
    sums = sums + swap(sums, "orb", 0)
    shards0, pay_b = lax.optimization_barrier(((sums * weights).astype(dtype), pay_b))
    got_b = swap(pay_b, "orb", 0)

    def gather():
        return double(shards0, "aux", bits)

    def nothing():
        half = jnp.zeros((aux // 2, 2, shard, width), dtype)
        return half, half

    near, far = lax.cond(used, gather, nothing)

    def whole(shape):
        return pl.BlockSpec(shape, lambda i, plan: (0,) * len(shape))

    def run(kernel, steps, specs, out_shape, out_specs, scratch, cost, mebi=16):
        return pl.pallas_call(
            kernel,
            out_shape=out_shape,
            grid_spec=pltpu.PrefetchScalarGridSpec(
                num_scalar_prefetch=1,
                grid=(steps,),
                in_specs=specs,
                out_specs=out_specs,
                scratch_shapes=scratch,
            ),
            compiler_params=pltpu.CompilerParams(vmem_limit_bytes=mebi * MEBI),
            cost_estimate=pl.CostEstimate(
                flops=cost * 2 * step * width * width,
                bytes_accessed=cost * step * width * 2,
                transcendentals=0,
            ),
        )

    amp = pltpu.VMEM((width, width), dtype)
    back = run(
        back_kernel,
        1,
        [
            whole(near.shape),
            whole(far.shape),
            pl.BlockSpec((2, step, width), lambda i, plan: (0, 0, 0)),
        ],
        array(step, width),
        whole((step, width)),
        [amp, amp],
        1,
    )(plan, near, far, factors)
    got_back = swap(back, "orb", 0)

    def at(helper_block, owner_block):
        return pl.BlockSpec(
            (step, width),
            lambda i, plan: (
                jnp.where(plan[HELPS] == 1, helper_block(i), owner_block(i)),
                0,
            ),
        )

    def clip(low, high, shift):
        return lambda i: jnp.clip(i + shift, low, high)

    none = clip(0, 0, 0)
    pieces = pl.BlockSpec((2, step, width), lambda i, plan: (0, i, 0))
    gamma = run(
        last_kernel,
        4,
        [whole(near01.shape), whole(far01.shape), whole(near.shape), whole(far.shape)]
        + [at(clip(0, 2, 0), clip(0, 1, -2)), at(none, none), at(none, clip(2, 2, 0)), pieces],
        array(*factors.shape),
        pieces,
        [amp, amp, amp],
        12,
    )(plan, near01, far01, near, far, got1, got_a, got1, factors)

    gamma = call(
        functools.partial(late_kernel, step),
        array(*factors.shape),
        [SMEM_SPEC, VMEM_SPEC, VMEM_SPEC, VMEM_SPEC, HBM_SPEC],
        HBM_SPEC,
        [amp, amp, pltpu.VMEM((step, width), dtype), dma],
        1,
        input_output_aliases={4: 0},
    )(plan, near, far, got_b, gamma)
    return call(
        functools.partial(put_kernel, step),
        array(*factors.shape),
        [SMEM_SPEC, VMEM_SPEC, HBM_SPEC],
        HBM_SPEC,
        [dma],
        input_output_aliases={2: 0},
    )(plan, got_back, gamma)


def shards(factors, occ_energy, virt_energy, tile_table):
    groups = lax.axis_size("orb")
    aux = lax.axis_size("aux")
    simple = groups == 2 and factors.shape[0] == 2 and tile_table.shape[0] <= CAP
    width = factors.shape[2]
    whole_shards = aux & (aux - 1) == 0 and width % (32 * aux) == 0
    if simple and whole_shards and factors.shape[1] % 128 == 0:
        return two_groups(factors, occ_energy, virt_energy, tile_table)
    return general(factors, occ_energy, virt_energy, tile_table)


def solution(mesh):
    return jax.shard_map(
        shards,
        mesh=mesh,
        in_specs=(P("orb", "aux", None), P(), P(), P()),
        out_specs=P("orb", "aux", None),
        check_vma=False,
    )
```

```python
import functools

import jax
import jax.numpy as jnp
from jax import lax
from jax.experimental import pallas as pl
from jax.experimental.pallas import tpu as pltpu
from jax.sharding import PartitionSpec as P

CAP = 4
WIRE = jnp.bfloat16
HELPS, FOREIGN, PLACE, COUNTS, LOW, PARTNER = 0, 1, 2, 3, 6, 7
MEBI = 1024 * 1024
SMEM_SPEC = pl.BlockSpec(memory_space=pltpu.SMEM)
HBM_SPEC = pl.BlockSpec(memory_space=pltpu.HBM)
VMEM_SPEC = pl.BlockSpec(memory_space=pltpu.VMEM)


def general(factors, occ_energy, virt_energy, tile_table):
    owned = factors.shape[0]
    width = factors.shape[2]
    tiles = tile_table.shape[0]
    groups = lax.axis_size("orb")
    mine = lax.axis_index("orb")
    first = tile_table[:, 0]
    second = tile_table[:, 1]
    helper = tile_table[:, 2]
    block_ids = jnp.arange(owned * groups, dtype=jnp.int32)
    group_ids = jnp.arange(groups, dtype=jnp.int32)
    local_ids = jnp.arange(owned, dtype=jnp.int32)
    touched = (
        (first[:, None] == block_ids[None, :]) | (second[:, None] == block_ids[None, :])
    ).astype(jnp.int32)
    helped = (helper[:, None] == group_ids[None, :]).astype(jnp.int32)
    usage = jnp.sum(helped[:, :, None] * touched[:, None, :], axis=0) > 0
    usage = usage.reshape(groups, groups, owned).astype(jnp.int32)
    own_usage = jnp.take(usage, mine, axis=1)
    send_pick = jnp.sum(own_usage * local_ids[None, :], axis=1)
    outgoing = jnp.stack(
        [
            lax.dynamic_index_in_dim(factors, send_pick[group], 0, keepdims=False)
            for group in range(groups)
        ]
    )
    incoming = lax.all_to_all(outgoing, "orb", split_axis=0, concat_axis=0, tiled=True)
    store = jnp.concatenate([factors, incoming], axis=0)

    def position(block):
        owner = block // owned
        return jnp.where(owner == mine, block % owned, owned + owner)

    is_mine = (helper == mine).astype(jnp.int32)
    tile_ids = jnp.arange(tiles, dtype=jnp.int32)
    earlier = (tile_ids[None, :] < tile_ids[:, None]).astype(jnp.int32)
    rank = jnp.sum(earlier * is_mine[None, :], axis=1)
    slot_ids = jnp.arange(CAP, dtype=jnp.int32)
    picked = is_mine[None, :] * (rank[None, :] == slot_ids[:, None]).astype(jnp.int32)
    valid = jnp.sum(picked, axis=1)
    tile_p = jnp.sum(picked * first[None, :], axis=1)
    tile_q = jnp.sum(picked * second[None, :], axis=1)
    place_p = position(tile_p)
    place_q = position(tile_q)
    energy_p = jnp.take(virt_energy, tile_p, axis=0)
    energy_q = jnp.take(virt_energy, tile_q, axis=0)
    occ_sum = jnp.take(occ_energy, tile_p) + jnp.take(occ_energy, tile_q)
    denominators = energy_p[:, :, None] + energy_q[:, None, :] - occ_sum[:, None, None]

    def partners(slot):
        block_p = lax.dynamic_index_in_dim(store, place_p[slot], 0, keepdims=False)
        block_q = lax.dynamic_index_in_dim(store, place_q[slot], 0, keepdims=False)
        return (block_p, block_q)

    def fill(slot, buffer):
        block_p, block_q = partners(slot)
        return lax.dynamic_update_index_in_dim(buffer, outer(block_p, block_q), slot, 0)

    buffer = lax.fori_loop(0, CAP, fill, jnp.zeros((CAP, width, width), jnp.float32))
    summed = lax.psum(buffer, "aux")
    all_amps = (summed / denominators).astype(jnp.bfloat16)

    def apply_all(slot, gathered):
        block_p, block_q = partners(slot)
        amplitudes = lax.dynamic_index_in_dim(all_amps, slot, 0, keepdims=False)
        amplitudes = jnp.where(valid[slot] > 0, amplitudes, jnp.zeros_like(amplitudes))
        gathered = gathered.at[place_p[slot]].add(right_t(block_q, amplitudes))
        return gathered.at[place_q[slot]].add(right(block_p, amplitudes))

    gathered = lax.fori_loop(0, CAP, apply_all, jnp.zeros(store.shape, jnp.float32))
    helper_part = gathered[owned:].astype(jnp.bfloat16)
    returned = lax.all_to_all(helper_part, "orb", split_axis=0, concat_axis=0, tiled=True)
    landing = (send_pick[:, None] == local_ids[None, :]).astype(jnp.float32)
    gamma = gathered[:owned] + jnp.einsum(
        "dj,dav->jav", landing, returned.astype(jnp.float32), precision=lax.Precision.HIGHEST
    )
    return gamma.astype(jnp.bfloat16)


def outer(a, b):
    return lax.dot_general(a, b, (((0,), (0,)), ((), ())), preferred_element_type=jnp.float32)


def right(a, m):
    return jnp.dot(a, m, preferred_element_type=jnp.float32)


def right_t(a, m):
    return lax.dot_general(a, m, (((1,), (1,)), ((), ())), preferred_element_type=jnp.float32)


def swap(value, axis, bit):
    size = lax.axis_size(axis)
    return lax.ppermute(value, axis, [(i, i ^ (1 << bit)) for i in range(size)])


def halve(kept, sent, axis, wires):
    me = lax.axis_index(axis)
    part = kept + swap(sent, axis, 0).astype(jnp.float32)
    for bit, wire in list(enumerate(wires))[1:]:
        high = ((me >> bit) & 1) == 1
        half = part.shape[1] // 2
        low_rows, high_rows = part[:, :half], part[:, half:]
        sent = jnp.where(high, low_rows, high_rows).astype(wire)
        kept = jnp.where(high, high_rows, low_rows)
        part = kept + swap(sent, axis, bit).astype(jnp.float32)
    return part


def double(part, axis, bits):
    part = part[None]
    for bit in reversed(range(1, bits)):
        part = jnp.concatenate([part, swap(part, axis, bit)], axis=0)
    return part, swap(part, axis, 0)


def after(value, *others):
    return lax.optimization_barrier((value, *others))[0]


def start_all(copies):
    for copy in copies:
        copy.start()


def wait_all(copies):
    for copy in copies:
        copy.wait()


def rows_at(unit, start, size):
    return pl.ds(pl.multiple_of(start * unit, unit), size * unit)


def plan_kernel(tiles, bits, step, table, factors, plan, pay, sems):
    helper = table[0, 2]
    helps = (lax.axis_index("orb") == helper).astype(jnp.int32)
    low, foreign_low = helper * 2, (1 - helper) * 2
    foreign = jnp.int32(0)
    for t in range(tiles):
        named = (table[t, 0] == foreign_low + 1) | (table[t, 1] == foreign_low + 1)
        foreign = foreign | named.astype(jnp.int32)
    b0, b1 = jnp.where(helps == 1, 0, foreign), jnp.where(helps == 1, 1, foreign)
    copies = [
        pltpu.make_async_copy(
            factors.at[b0, rows_at(step, 2 * helps, 2)], pay.at[pl.ds(0, 2 * step)], sems.at[0]
        ),
        pltpu.make_async_copy(
            factors.at[b1, rows_at(step, 2 + helps, 1)], pay.at[pl.ds(2 * step, step)], sems.at[1]
        ),
    ]
    start_all(copies)
    me = lax.axis_index("aux")
    place = jnp.int32(0)
    for bit in range(bits):
        place = place * 2 + ((me >> bit) & 1)
    plan[HELPS], plan[FOREIGN], plan[PLACE] = helps, foreign, place
    plan[LOW], plan[PARTNER] = low, foreign_low + foreign
    pairs = ((low, low + 1), (low, foreign_low + foreign), (low + 1, foreign_low + foreign))
    for n, (a, b) in enumerate(pairs):
        count = jnp.int32(0)
        for t in range(tiles):
            p, q = table[t, 0], table[t, 1]
            same = ((p == a) & (q == b)) | ((p == b) & (q == a))
            count = count + same.astype(jnp.int32)
        plan[COUNTS + n] = count
    wait_all(copies)


def weigh_kernel(step, plan, occ, virt, factors, own_weight, weights, pay_a, sems):
    helps, foreign = plan[HELPS], plan[FOREIGN]
    b0, b1 = jnp.where(helps == 1, 0, foreign), jnp.where(helps == 1, 1, foreign)
    copies = [
        pltpu.make_async_copy(
            factors.at[block, rows_at(step, start, 1)], pay_a.at[pl.ds(n * step, step)], sems.at[n]
        )
        for n, (block, start) in enumerate(((b1, 3 - helps), (b0, 1)))
    ]
    start_all(copies)
    low, partner = plan[LOW], plan[PARTNER]
    _, shard, width = own_weight.shape
    row = lax.broadcasted_iota(jnp.int32, (shard, width), 0)
    column = lax.broadcasted_iota(jnp.int32, (shard, width), 1)
    mine = column == row + plan[PLACE] * shard
    pairs = ((low, low + 1, own_weight, 0), (low, partner, weights, 0), (low + 1, partner, weights, 1))
    for n, (a, b, out, slot) in enumerate(pairs):
        virt_a = jnp.sum(jnp.where(mine, virt[pl.ds(a, 1), :], 0.0), axis=1, keepdims=True)
        denominators = virt_a + virt[pl.ds(b, 1), :] - occ[a] - occ[b]
        out[slot] = plan[COUNTS + n].astype(jnp.float32) / denominators
    wait_all(copies)


def pack_kernel(unit, plan, factors, pay_b, sems):
    helps, foreign = plan[HELPS], plan[FOREIGN]
    b0, b1 = jnp.where(helps == 1, 0, foreign), jnp.where(helps == 1, 1, foreign)
    copies = [
        pltpu.make_async_copy(
            factors.at[block, pl.ds(start * unit, size * unit)],
            pay_b.at[pl.ds(to * unit, size * unit)],
            sems.at[n],
        )
        for n, (block, start, size, to) in enumerate(((b1, 2, 2, 0), (b0, 1, 1, 2), (b1, 1, 1, 3)))
    ]
    start_all(copies)
    wait_all(copies)


def split_halves(acc, pair, kept, sent, core):
    half = kept.shape[1]
    kept[pair] = acc[pl.ds(pl.multiple_of(core * half, half), half), :]
    other = acc[pl.ds(pl.multiple_of((1 - core) * half, half), half), :]
    sent[pair] = other.astype(sent.dtype)


def own_kernel(step, plan, factors, kept, sent, rows, acc, sems):
    del plan
    copies = [
        pltpu.make_async_copy(
            factors.at[:, pl.ds(n * step, step)], rows.at[:, pl.ds(n * step, step)], sems.at[n]
        )
        for n in range(4)
    ]
    start_all(copies)
    for n in range(4):
        copies[n].wait()
        term = outer(rows[0, n * step : (n + 1) * step], rows[1, n * step : (n + 1) * step])
        acc[...] = term if n == 0 else acc[...] + term
    split_halves(acc, 0, kept, sent, lax.axis_index("aux") & 1)


def pair_kernel(step, plan, factors, got, kept, sent, rows0, rows1, acc0, acc1, sems):
    helps, foreign = plan[HELPS], plan[FOREIGN]
    b0, b1 = jnp.where(helps == 1, 0, foreign), jnp.where(helps == 1, 1, foreign)
    copies0 = [
        pltpu.make_async_copy(
            factors.at[b0, rows_at(step, jnp.where(helps == 1, n, 2 + n), 1)],
            rows0.at[pl.ds(n * step, step)],
            sems.at[n],
        )
        for n in range(2)
    ]
    copies1 = [
        pltpu.make_async_copy(
            factors.at[b1, rows_at(step, jnp.where(helps == 1, n, 3), 1)],
            rows1.at[pl.ds(n * step, step)],
            sems.at[2 + n],
        )
        for n in range(3)
    ]
    start_all(copies0 + copies1)

    def cut(ref, n):
        return ref[n * step : (n + 1) * step]

    copies0[0].wait()

    @pl.when(helps == 1)
    def _():
        acc0[...] = outer(cut(rows0, 0), cut(got, 0))

    @pl.when(helps == 0)
    def _():
        acc0[...] = outer(cut(got, 0), cut(rows0, 0))

    copies0[1].wait()

    @pl.when(helps == 1)
    def _():
        acc0[...] += outer(cut(rows0, 1), cut(got, 1))

    @pl.when(helps == 0)
    def _():
        acc0[...] += outer(cut(got, 1), cut(rows0, 1))

    wait_all(copies1)

    @pl.when(helps == 1)
    def _():
        acc1[...] = outer(cut(rows1, 0), cut(got, 0)) + outer(cut(rows1, 1), cut(got, 1))
        acc1[...] += outer(cut(rows1, 2), cut(got, 2))

    @pl.when(helps == 0)
    def _():
        acc1[...] = outer(cut(got, 2), cut(rows1, 2))

    core = lax.axis_index("aux") & 1
    split_halves(acc0, 0, kept, sent, core)
    split_halves(acc1, 1, kept, sent, core)


def arrange(plan, near, far, pair, out):
    count, _, shard, _ = near.shape
    for source, base in ((near, 0), (far, count)):
        for n in range(count):
            row = pl.multiple_of((plan[PLACE] ^ (base + n)) * shard, shard)
            out[pl.ds(row, shard), :] = source[n, pair]


def back_kernel(plan, near, far, blocks, back, amp0, amp1):
    arrange(plan, near, far, 0, amp0)
    arrange(plan, near, far, 1, amp1)
    total = right(blocks[0], amp0[...]) + right(blocks[1], amp1[...])
    back[...] = total.astype(back.dtype)


def last_kernel(plan, near01, far01, near, far, x, a, y, block0, block1, out, amps0, amps1):
    seg = pl.program_id(0)
    helps = plan[HELPS] == 1
    width = block0.shape[2]

    @pl.when((seg == 0) & helps)
    def _():
        arrange(plan, near01, far01, 0, amps1.at[:width])
        amps0[:width] = amps1[:width].T
        arrange(plan, near, far, 0, amps1.at[width:])
        amps0[width:] = amps1[width:].T
        arrange(plan, near, far, 1, amps1.at[width:])
        amps1[width:] = amps1[width:].T

    @pl.when((seg == 0) & jnp.logical_not(helps))
    def _():
        arrange(plan, near, far, 0, amps0.at[:width])
        arrange(plan, near, far, 1, amps0.at[width:])

    @pl.when(helps)
    def _():
        foreign = jnp.where(seg < 3, x[...], a[...])
        rows0 = jnp.concatenate([block1[0], foreign], axis=1)
        rows1 = jnp.concatenate([block0[0], foreign], axis=1)
        out[0] = right(rows0, amps0[...]).astype(out.dtype)
        out[1] = right(rows1, amps1[...]).astype(out.dtype)

    @pl.when(jnp.logical_not(helps))
    def _():
        out[...] = jnp.zeros_like(out)

    @pl.when(jnp.logical_not(helps) & (seg >= 2))
    def _():
        rows = jnp.concatenate([x[...], jnp.where(seg < 3, a[...], y[...])], axis=1)
        out[plan[FOREIGN]] = right(rows, amps0[...]).astype(out.dtype)


def late_kernel(unit, plan, near, far, got_a, got_b, gamma_in, gamma, amp0, amp1, rows, sem):
    @pl.when(plan[HELPS] == 0)
    def _():
        arrange(plan, near, far, 0, amp0)
        arrange(plan, near, far, 1, amp1)
        total = right(got_b[2 * unit : 3 * unit], amp0[...]) + right(got_b[3 * unit :], amp1[...])
        rows[:unit] = total.astype(rows.dtype)
        total = right(got_a[2 * unit :], amp0[...]) + right(got_b[: 2 * unit], amp1[...])
        rows[unit:] = total.astype(rows.dtype)
        copy = pltpu.make_async_copy(rows, gamma.at[plan[FOREIGN], pl.ds(unit, 3 * unit)], sem)
        copy.start()
        copy.wait()


def put_kernel(unit, plan, back, gamma_in, gamma, sem):
    @pl.when(plan[HELPS] == 0)
    def _():
        copy = pltpu.make_async_copy(back, gamma.at[plan[FOREIGN], pl.ds(0, unit)], sem)
        copy.start()
        copy.wait()


def two_groups(factors, occ_energy, virt_energy, tile_table):
    owned, rows, width = factors.shape
    aux = lax.axis_size("aux")
    bits = aux.bit_length() - 1
    step, unit = rows // 4, rows // 8
    shard = width // aux
    wires = [jnp.float32] + [WIRE] * (bits - 1)
    dtype = factors.dtype
    dma = pltpu.SemaphoreType.DMA

    def array(*shape, dtype=dtype):
        return jax.ShapeDtypeStruct(shape, dtype)

    def call(kernel, out_shape, in_specs, out_specs, scratch, cost=0, mebi=16, **options):
        return pl.pallas_call(
            kernel,
            out_shape=out_shape,
            in_specs=in_specs,
            out_specs=out_specs,
            scratch_shapes=scratch,
            compiler_params=pltpu.CompilerParams(vmem_limit_bytes=mebi * MEBI),
            cost_estimate=pl.CostEstimate(
                flops=cost * 2 * step * width * width,
                bytes_accessed=2 * step * width * 2,
                transcendentals=0,
            ),
            **options,
        )

    plan, pay1 = call(
        functools.partial(plan_kernel, tile_table.shape[0], bits, step),
        (array(8, dtype=jnp.int32), array(3 * step, width)),
        [SMEM_SPEC, HBM_SPEC],
        (SMEM_SPEC, VMEM_SPEC),
        [dma((2,))],
        mebi=61,
    )(tile_table, factors)
    got1 = swap(pay1, "orb", 0)

    def halves(pairs):
        kept = array(pairs, width // 2, width, dtype=jnp.float32)
        return kept, array(pairs, width // 2, width, dtype=wires[0])

    square = pltpu.VMEM((width, width), jnp.float32)

    def prepare():
        return call(
            functools.partial(weigh_kernel, step),
            (
                array(1, shard, width, dtype=jnp.float32),
                array(2, shard, width, dtype=jnp.float32),
                array(2 * step, width),
            ),
            [SMEM_SPEC, SMEM_SPEC, VMEM_SPEC, HBM_SPEC],
            (VMEM_SPEC, VMEM_SPEC, VMEM_SPEC),
            [dma((2,))],
        )(plan, occ_energy, virt_energy, factors)

    def own_chain():
        kept, sent = call(
            functools.partial(own_kernel, step),
            halves(1),
            [SMEM_SPEC, HBM_SPEC],
            (VMEM_SPEC, VMEM_SPEC),
            [pltpu.VMEM(factors.shape, dtype), square, dma((4,))],
            4,
        )(plan, factors)
        own_weight, weights, pay_a = prepare()
        sum01 = halve(kept, sent, "aux", wires)
        return *double((sum01 * own_weight).astype(dtype), "aux", bits), weights, pay_a

    def no_chain():
        half = jnp.zeros((aux // 2, 1, shard, width), dtype)
        return half, half, *prepare()[1:]

    near01, far01, weights, pay_a = lax.cond(plan[COUNTS] > 0, own_chain, no_chain)
    got1, near01, far01, weights, pay_a = lax.optimization_barrier(
        (got1, near01, far01, weights, pay_a)
    )
    got_a = swap(pay_a, "orb", 0)

    def pair_chain():
        kept, sent = call(
            functools.partial(pair_kernel, step),
            halves(2),
            [SMEM_SPEC, HBM_SPEC, VMEM_SPEC],
            (VMEM_SPEC, VMEM_SPEC),
            [
                pltpu.VMEM((2 * step, width), dtype),
                pltpu.VMEM((3 * step, width), dtype),
                square,
                square,
                dma((5,)),
            ],
            5,
        )(plan, factors, got1)
        return halve(kept, sent, "aux", wires), pack(after(plan, kept))

    def pack(plan):
        return call(
            functools.partial(pack_kernel, unit),
            array(4 * unit, width),
            [SMEM_SPEC, HBM_SPEC],
            VMEM_SPEC,
            [dma((3,))],
        )(plan, factors)

    used = plan[COUNTS + 1] + plan[COUNTS + 2] > 0
    sums, pay_b = lax.cond(
        used, pair_chain, lambda: (jnp.zeros((2, shard, width), jnp.float32), pack(plan))
    )
    sums, got_a, pay_b = lax.optimization_barrier((sums, got_a, pay_b))
    sums = sums + swap(sums, "orb", 0)
    shards0, pay_b = lax.optimization_barrier(((sums * weights).astype(dtype), pay_b))
    got_b = swap(pay_b, "orb", 0)

    def gather():
        return double(shards0, "aux", bits)

    def nothing():
        half = jnp.zeros((aux // 2, 2, shard, width), dtype)
        return half, half

    near, far = lax.cond(used, gather, nothing)

    def whole(shape):
        return pl.BlockSpec(shape, lambda i, plan: (0,) * len(shape))

    def run(kernel, steps, specs, out_shape, out_specs, scratch, cost, mebi=16):
        return pl.pallas_call(
            kernel,
            out_shape=out_shape,
            grid_spec=pltpu.PrefetchScalarGridSpec(
                num_scalar_prefetch=1,
                grid=(steps,),
                in_specs=specs,
                out_specs=out_specs,
                scratch_shapes=scratch,
            ),
            compiler_params=pltpu.CompilerParams(vmem_limit_bytes=mebi * MEBI),
            cost_estimate=pl.CostEstimate(
                flops=cost * 2 * step * width * width,
                bytes_accessed=cost * step * width * 2,
                transcendentals=0,
            ),
        )

    amp = pltpu.VMEM((width, width), dtype)
    back = run(
        back_kernel,
        1,
        [
            whole(near.shape),
            whole(far.shape),
            pl.BlockSpec((2, unit, width), lambda i, plan: (0, 0, 0)),
        ],
        array(unit, width),
        whole((unit, width)),
        [amp, amp],
        1,
    )(plan, near, far, factors)
    got_back = swap(back, "orb", 0)

    def at(helper_block, owner_block):
        return pl.BlockSpec(
            (step, width),
            lambda i, plan: (
                jnp.where(plan[HELPS] == 1, helper_block(i), owner_block(i)),
                0,
            ),
        )

    def clip(low, high, shift):
        return lambda i: jnp.clip(i + shift, low, high)

    none = clip(0, 0, 0)
    pieces = pl.BlockSpec((2, step, width), lambda i, plan: (0, i, 0))
    gamma = run(
        last_kernel,
        4,
        [whole(near01.shape), whole(far01.shape), whole(near.shape), whole(far.shape)]
        + [at(clip(0, 2, 0), clip(0, 1, -2)), at(none, none), at(none, clip(2, 2, 0))]
        + [
            pl.BlockSpec((1, step, width), lambda i, plan: (0, i, 0)),
            pl.BlockSpec((1, step, width), lambda i, plan: (1, i, 0)),
        ],
        array(*factors.shape),
        pieces,
        [pltpu.VMEM((2 * width, width), dtype)] * 2,
        12,
    )(plan, near01, far01, near, far, got1, got_a, got1, factors, factors)

    gamma = call(
        functools.partial(late_kernel, unit),
        array(*factors.shape),
        [SMEM_SPEC, VMEM_SPEC, VMEM_SPEC, VMEM_SPEC, VMEM_SPEC, HBM_SPEC],
        HBM_SPEC,
        [amp, amp, pltpu.VMEM((3 * unit, width), dtype), dma],
        1,
        input_output_aliases={5: 0},
    )(plan, near, far, got_a, got_b, gamma)
    return call(
        functools.partial(put_kernel, unit),
        array(*factors.shape),
        [SMEM_SPEC, VMEM_SPEC, HBM_SPEC],
        HBM_SPEC,
        [dma],
        input_output_aliases={2: 0},
    )(plan, got_back, gamma)


def shards(factors, occ_energy, virt_energy, tile_table):
    groups = lax.axis_size("orb")
    aux = lax.axis_size("aux")
    simple = groups == 2 and factors.shape[0] == 2 and tile_table.shape[0] <= CAP
    width = factors.shape[2]
    whole_shards = aux & (aux - 1) == 0 and width % (32 * aux) == 0
    if simple and whole_shards and factors.shape[1] % 128 == 0:
        return two_groups(factors, occ_energy, virt_energy, tile_table)
    return general(factors, occ_energy, virt_energy, tile_table)


def solution(mesh):
    return jax.shard_map(
        shards,
        mesh=mesh,
        in_specs=(P("orb", "aux", None), P(), P(), P()),
        out_specs=P("orb", "aux", None),
        check_vma=False,
    )
```

```python
import functools

import jax
import jax.numpy as jnp
from jax import lax
from jax.experimental import pallas as pl
from jax.experimental.pallas import tpu as pltpu
from jax.sharding import PartitionSpec as P

CAP = 4
WIRE = jnp.bfloat16
HELPS, FOREIGN, PLACE, COUNTS, LOW, PARTNER = 0, 1, 2, 3, 6, 7
MEBI = 1024 * 1024
SMEM_SPEC = pl.BlockSpec(memory_space=pltpu.SMEM)
HBM_SPEC = pl.BlockSpec(memory_space=pltpu.HBM)
VMEM_SPEC = pl.BlockSpec(memory_space=pltpu.VMEM)


def general(factors, occ_energy, virt_energy, tile_table):
    owned = factors.shape[0]
    width = factors.shape[2]
    tiles = tile_table.shape[0]
    groups = lax.axis_size("orb")
    mine = lax.axis_index("orb")
    first = tile_table[:, 0]
    second = tile_table[:, 1]
    helper = tile_table[:, 2]
    block_ids = jnp.arange(owned * groups, dtype=jnp.int32)
    group_ids = jnp.arange(groups, dtype=jnp.int32)
    local_ids = jnp.arange(owned, dtype=jnp.int32)
    touched = (
        (first[:, None] == block_ids[None, :]) | (second[:, None] == block_ids[None, :])
    ).astype(jnp.int32)
    helped = (helper[:, None] == group_ids[None, :]).astype(jnp.int32)
    usage = jnp.sum(helped[:, :, None] * touched[:, None, :], axis=0) > 0
    usage = usage.reshape(groups, groups, owned).astype(jnp.int32)
    own_usage = jnp.take(usage, mine, axis=1)
    send_pick = jnp.sum(own_usage * local_ids[None, :], axis=1)
    outgoing = jnp.stack(
        [
            lax.dynamic_index_in_dim(factors, send_pick[group], 0, keepdims=False)
            for group in range(groups)
        ]
    )
    incoming = lax.all_to_all(outgoing, "orb", split_axis=0, concat_axis=0, tiled=True)
    store = jnp.concatenate([factors, incoming], axis=0)

    def position(block):
        owner = block // owned
        return jnp.where(owner == mine, block % owned, owned + owner)

    is_mine = (helper == mine).astype(jnp.int32)
    tile_ids = jnp.arange(tiles, dtype=jnp.int32)
    earlier = (tile_ids[None, :] < tile_ids[:, None]).astype(jnp.int32)
    rank = jnp.sum(earlier * is_mine[None, :], axis=1)
    slot_ids = jnp.arange(CAP, dtype=jnp.int32)
    picked = is_mine[None, :] * (rank[None, :] == slot_ids[:, None]).astype(jnp.int32)
    valid = jnp.sum(picked, axis=1)
    tile_p = jnp.sum(picked * first[None, :], axis=1)
    tile_q = jnp.sum(picked * second[None, :], axis=1)
    place_p = position(tile_p)
    place_q = position(tile_q)
    energy_p = jnp.take(virt_energy, tile_p, axis=0)
    energy_q = jnp.take(virt_energy, tile_q, axis=0)
    occ_sum = jnp.take(occ_energy, tile_p) + jnp.take(occ_energy, tile_q)
    denominators = energy_p[:, :, None] + energy_q[:, None, :] - occ_sum[:, None, None]

    def partners(slot):
        block_p = lax.dynamic_index_in_dim(store, place_p[slot], 0, keepdims=False)
        block_q = lax.dynamic_index_in_dim(store, place_q[slot], 0, keepdims=False)
        return (block_p, block_q)

    def fill(slot, buffer):
        block_p, block_q = partners(slot)
        return lax.dynamic_update_index_in_dim(buffer, outer(block_p, block_q), slot, 0)

    buffer = lax.fori_loop(0, CAP, fill, jnp.zeros((CAP, width, width), jnp.float32))
    summed = lax.psum(buffer, "aux")
    all_amps = (summed / denominators).astype(jnp.bfloat16)

    def apply_all(slot, gathered):
        block_p, block_q = partners(slot)
        amplitudes = lax.dynamic_index_in_dim(all_amps, slot, 0, keepdims=False)
        amplitudes = jnp.where(valid[slot] > 0, amplitudes, jnp.zeros_like(amplitudes))
        gathered = gathered.at[place_p[slot]].add(right_t(block_q, amplitudes))
        return gathered.at[place_q[slot]].add(right(block_p, amplitudes))

    gathered = lax.fori_loop(0, CAP, apply_all, jnp.zeros(store.shape, jnp.float32))
    helper_part = gathered[owned:].astype(jnp.bfloat16)
    returned = lax.all_to_all(helper_part, "orb", split_axis=0, concat_axis=0, tiled=True)
    landing = (send_pick[:, None] == local_ids[None, :]).astype(jnp.float32)
    gamma = gathered[:owned] + jnp.einsum(
        "dj,dav->jav", landing, returned.astype(jnp.float32), precision=lax.Precision.HIGHEST
    )
    return gamma.astype(jnp.bfloat16)


def outer(a, b):
    return lax.dot_general(a, b, (((0,), (0,)), ((), ())), preferred_element_type=jnp.float32)


def right(a, m):
    return jnp.dot(a, m, preferred_element_type=jnp.float32)


def right_t(a, m):
    return lax.dot_general(a, m, (((1,), (1,)), ((), ())), preferred_element_type=jnp.float32)


def swap(value, axis, bit):
    size = lax.axis_size(axis)
    return lax.ppermute(value, axis, [(i, i ^ (1 << bit)) for i in range(size)])


def halve(kept, sent, axis, wires):
    me = lax.axis_index(axis)
    part = kept + swap(sent, axis, 0).astype(jnp.float32)
    for bit, wire in list(enumerate(wires))[1:]:
        high = ((me >> bit) & 1) == 1
        half = part.shape[1] // 2
        low_rows, high_rows = part[:, :half], part[:, half:]
        sent = jnp.where(high, low_rows, high_rows).astype(wire)
        kept = jnp.where(high, high_rows, low_rows)
        part = kept + swap(sent, axis, bit).astype(jnp.float32)
    return part


def widen(part, axis, bits):
    for bit in bits:
        part = jnp.concatenate([part, swap(part, axis, bit)], axis=0)
    return part


def double(part, axis, bits):
    part = widen(part, axis, reversed(range(1, bits)))
    return part, swap(part, axis, 0)


def after(value, *others):
    return lax.optimization_barrier((value, *others))[0]


def start_all(copies):
    for copy in copies:
        copy.start()


def wait_all(copies):
    for copy in copies:
        copy.wait()


def staged(source, stage, target, sems):
    first = pltpu.make_async_copy(source, stage, sems.at[0])
    return first, pltpu.make_async_copy(stage, target, sems.at[1])


def relay(copies):
    for first, second in copies:
        first.wait()
        second.start()


def rows_at(unit, start, size):
    return pl.ds(pl.multiple_of(start * unit, unit), size * unit)


def plan_kernel(tiles, bits, step, table, factors, plan, pay, stage, sems):
    helper = table[0, 2]
    helps = (lax.axis_index("orb") == helper).astype(jnp.int32)
    low, foreign_low = helper * 2, (1 - helper) * 2
    foreign = jnp.int32(0)
    for t in range(tiles):
        named = (table[t, 0] == foreign_low + 1) | (table[t, 1] == foreign_low + 1)
        foreign = foreign | named.astype(jnp.int32)
    b0, b1 = jnp.where(helps == 1, 0, foreign), jnp.where(helps == 1, 1, foreign)
    sources = ((b0, 2 * helps), (b0, 2 * helps + 1), (b1, 2 + helps))
    copies = [
        staged(
            factors.at[block, rows_at(step, start, 1)],
            stage.at[pl.ds(n * step, step)],
            pay.at[pl.ds(n * step, step)],
            sems.at[n],
        )
        for n, (block, start) in enumerate(sources)
    ]
    start_all(first for first, _ in copies)
    me = lax.axis_index("aux")
    place = jnp.int32(0)
    for bit in range(bits):
        place = place * 2 + ((me >> bit) & 1)
    plan[HELPS], plan[FOREIGN], plan[PLACE] = helps, foreign, place
    plan[LOW], plan[PARTNER] = low, foreign_low + foreign
    pairs = ((low, low + 1), (low, foreign_low + foreign), (low + 1, foreign_low + foreign))
    for n, (a, b) in enumerate(pairs):
        count = jnp.int32(0)
        for t in range(tiles):
            p, q = table[t, 0], table[t, 1]
            same = ((p == a) & (q == b)) | ((p == b) & (q == a))
            count = count + same.astype(jnp.int32)
        plan[COUNTS + n] = count
    relay(copies)
    wait_all(second for _, second in copies)


def weigh_kernel(step, plan, occ, virt, factors, own_weight, weights, pay_a, stage, sems):
    helps, foreign = plan[HELPS], plan[FOREIGN]
    b0, b1 = jnp.where(helps == 1, 0, foreign), jnp.where(helps == 1, 1, foreign)
    copies = [
        staged(
            factors.at[block, rows_at(step, start, 1)],
            stage.at[pl.ds(n * step, step)],
            pay_a.at[pl.ds(n * step, step)],
            sems.at[n],
        )
        for n, (block, start) in enumerate(((b1, 3 - helps), (b0, 1)))
    ]
    start_all(first for first, _ in copies)
    low, partner = plan[LOW], plan[PARTNER]
    _, shard, width = own_weight.shape
    row = lax.broadcasted_iota(jnp.int32, (shard, width), 0)
    column = lax.broadcasted_iota(jnp.int32, (shard, width), 1)
    mine = column == row + plan[PLACE] * shard
    pairs = ((low, low + 1, own_weight, 0), (low, partner, weights, 0), (low + 1, partner, weights, 1))
    for n, (a, b, out, slot) in enumerate(pairs):
        virt_a = jnp.sum(jnp.where(mine, virt[pl.ds(a, 1), :], 0.0), axis=1, keepdims=True)
        denominators = virt_a + virt[pl.ds(b, 1), :] - occ[a] - occ[b]
        out[slot] = plan[COUNTS + n].astype(jnp.float32) / denominators
    relay(copies)
    wait_all(second for _, second in copies)


def third_rows(unit, plan, factors, pay_b, stage, sems):
    helps, foreign = plan[HELPS], plan[FOREIGN]
    b0, b1 = jnp.where(helps == 1, 0, foreign), jnp.where(helps == 1, 1, foreign)
    return [
        staged(
            factors.at[block, pl.ds(start * unit, size * unit)],
            stage.at[pl.ds(to * unit, size * unit)],
            pay_b.at[pl.ds(to * unit, size * unit)],
            sems.at[n],
        )
        for n, (block, start, size, to) in enumerate(((b1, 2, 2, 0), (b0, 1, 1, 2), (b1, 1, 1, 3)))
    ]


def pack_kernel(unit, plan, factors, pay_b, stage, sems):
    copies = third_rows(unit, plan, factors, pay_b, stage, sems)
    start_all(first for first, _ in copies)
    relay(copies)
    wait_all(second for _, second in copies)


def split_halves(acc, pair, kept, sent, core):
    half = kept.shape[1]
    kept[pair] = acc[pl.ds(pl.multiple_of(core * half, half), half), :]
    other = acc[pl.ds(pl.multiple_of((1 - core) * half, half), half), :]
    sent[pair] = other.astype(sent.dtype)


def own_kernel(step, plan, factors, kept, sent, rows, acc, sems):
    del plan
    copies = [
        pltpu.make_async_copy(
            factors.at[:, pl.ds(n * step, step)], rows.at[:, pl.ds(n * step, step)], sems.at[n]
        )
        for n in range(4)
    ]
    start_all(copies)
    for n in range(4):
        copies[n].wait()
        term = outer(rows[0, n * step : (n + 1) * step], rows[1, n * step : (n + 1) * step])
        acc[...] = term if n == 0 else acc[...] + term
    split_halves(acc, 0, kept, sent, lax.axis_index("aux") & 1)


def pair_kernel(
    step, plan, factors, got_hbm, kept, sent, pay_b, got, rows0, rows1, acc0, acc1, stage, sems, pay_sems
):
    helps, foreign = plan[HELPS], plan[FOREIGN]
    b0, b1 = jnp.where(helps == 1, 0, foreign), jnp.where(helps == 1, 1, foreign)

    def cut(ref, n):
        return ref[n * step : (n + 1) * step]

    def fetch(source, ref, n, slot):
        return pltpu.make_async_copy(source, ref.at[pl.ds(n * step, step)], sems.at[slot])

    gots = [fetch(got_hbm.at[pl.ds(n * step, step)], got, n, n) for n in range(3)]
    copies0 = [
        fetch(factors.at[b0, rows_at(step, jnp.where(helps == 1, n, 2 + n), 1)], rows0, n, 3 + n)
        for n in range(2)
    ]
    copies1 = [
        fetch(factors.at[b1, rows_at(step, jnp.where(helps == 1, n, 3), 1)], rows1, n, 5 + n)
        for n in range(3)
    ]
    start_all((gots[0], copies0[0], gots[1], copies0[1], gots[2], copies1[2], *copies1[:2]))
    pays = third_rows(step // 2, plan, factors, pay_b, stage, pay_sems)
    start_all(first for first, _ in pays)

    for n in range(2):
        wait_all((gots[n], copies0[n]))

        @pl.when(helps == 1)
        def _():
            term = outer(cut(rows0, n), cut(got, n))
            acc0[...] = term if n == 0 else acc0[...] + term

        @pl.when(helps == 0)
        def _():
            term = outer(cut(got, n), cut(rows0, n))
            acc0[...] = term if n == 0 else acc0[...] + term

    wait_all((gots[2], copies1[2]))

    @pl.when(helps == 1)
    def _():
        acc1[...] = outer(cut(rows1, 2), cut(got, 2))

    @pl.when(helps == 0)
    def _():
        acc1[...] = outer(cut(got, 2), cut(rows1, 2))

    wait_all(copies1[:2])
    relay(pays)

    @pl.when(helps == 1)
    def _():
        acc1[...] += outer(cut(rows1, 0), cut(got, 0)) + outer(cut(rows1, 1), cut(got, 1))

    core = lax.axis_index("aux") & 1
    split_halves(acc0, 0, kept, sent, core)
    split_halves(acc1, 1, kept, sent, core)
    wait_all(second for _, second in pays)


def arrange(plan, near, far, pair, out):
    count, _, shard, _ = near.shape
    for source, base in ((near, 0), (far, count)):
        for n in range(count):
            row = pl.multiple_of((plan[PLACE] ^ (base + n)) * shard, shard)
            out[pl.ds(row, shard), :] = source[n, pair]


def back_kernel(plan, near, far, blocks, back, amp0, amp1):
    arrange(plan, near, far, 0, amp0)
    arrange(plan, near, far, 1, amp1)
    total = right(blocks[0], amp0[...]) + right(blocks[1], amp1[...])
    back[...] = total.astype(back.dtype)


def last_kernel(
    step, plan, near01, far01, near, far, got1, got_a, got_b, factors, gamma, small, wide, rows, own, out, amps, ins, outs
):
    unit = step // 2
    width = out.shape[2]
    foreign = plan[FOREIGN]
    own_amp, amp0, amp1 = amps.at[0], amps.at[1], amps.at[2]

    def part(start, size):
        return pl.ds(start * unit, size * unit)

    def copy(source, target, slot):
        return pltpu.make_async_copy(source, target, ins.at[slot])

    gathered = [copy(near, wide.at[0], 0), copy(far, wide.at[1], 1)]

    @pl.when(plan[HELPS] == 1)
    def _():
        singles = [copy(near01, small.at[0], 2), copy(far01, small.at[1], 3)]
        sources = [got1.at[part(2 * n, 2)] for n in range(3)] + [got_a.at[part(0, 2)]]
        others = [copy(sources[n], rows.at[part(2 * n, 2)], 4 + n) for n in range(4)]
        mine = [copy(factors.at[:, part(2 * n, 2)], own.at[:, part(2 * n, 2)], 8 + n) for n in range(4)]
        start_all(singles + gathered)
        for n in range(4):
            start_all((mine[n], others[n]))
        wait_all(singles)
        arrange(plan, small.at[0], small.at[1], 0, own_amp)
        wait_all(gathered)
        arrange(plan, wide.at[0], wide.at[1], 0, amp0)
        arrange(plan, wide.at[0], wide.at[1], 1, amp1)
        results = []
        for n in range(4):
            wait_all((mine[n], others[n]))
            at = slice(n * step, (n + 1) * step)
            first = right_t(own[1, at], own_amp[...]) + right_t(rows[at], amp0[...])
            out[0, at] = first.astype(out.dtype)
            second = right(own[0, at], own_amp[...]) + right_t(rows[at], amp1[...])
            out[1, at] = second.astype(out.dtype)
            place = part(2 * n, 2)
            results.append(pltpu.make_async_copy(out.at[:, place], gamma.at[:, place], outs.at[n]))
            results[-1].start()
        wait_all(results)

    @pl.when(plan[HELPS] == 0)
    def _():
        others = [
            copy(got1, rows.at[part(0, 6)], 4),
            copy(got_a, rows.at[part(6, 4)], 5),
            copy(got_b, rows.at[part(10, 4)], 6),
        ]
        start_all(gathered + others)
        out[0] = jnp.zeros_like(out[0])
        results = [pltpu.make_async_copy(out.at[0], gamma.at[1 - foreign], outs.at[0])]
        results[0].start()
        wait_all(gathered)
        arrange(plan, wide.at[0], wide.at[1], 0, amp0)
        arrange(plan, wide.at[0], wide.at[1], 1, amp1)
        wait_all(others)
        pieces = ((6, 2, 2, 4), (4, 2, 0, 6), (2, 2, 8, 10), (1, 1, 12, 13))
        for n, (start, size, row0, row1) in enumerate(pieces):
            rows0 = rows[row0 * unit : (row0 + size) * unit]
            rows1 = rows[row1 * unit : (row1 + size) * unit]
            total = right(rows0, amp0[...]) + right(rows1, amp1[...])
            out[1, start * unit : (start + size) * unit] = total.astype(out.dtype)
            place = part(start, size)
            results.append(
                pltpu.make_async_copy(out.at[1, place], gamma.at[foreign, place], outs.at[1 + n])
            )
            results[-1].start()
        wait_all(results)


def put_kernel(unit, plan, back, gamma_in, gamma, sem):
    @pl.when(plan[HELPS] == 0)
    def _():
        copy = pltpu.make_async_copy(back, gamma.at[plan[FOREIGN], pl.ds(0, unit)], sem)
        copy.start()
        copy.wait()


def two_groups(factors, occ_energy, virt_energy, tile_table):
    owned, rows, width = factors.shape
    aux = lax.axis_size("aux")
    bits = aux.bit_length() - 1
    step, unit = rows // 4, rows // 8
    shard = width // aux
    wires = [WIRE] * bits
    dtype = factors.dtype
    dma = pltpu.SemaphoreType.DMA

    def array(*shape, dtype=dtype):
        return jax.ShapeDtypeStruct(shape, dtype)

    def call(kernel, out_shape, in_specs, out_specs, scratch, cost=0, mebi=16, **options):
        return pl.pallas_call(
            kernel,
            out_shape=out_shape,
            in_specs=in_specs,
            out_specs=out_specs,
            scratch_shapes=scratch,
            compiler_params=pltpu.CompilerParams(vmem_limit_bytes=mebi * MEBI),
            cost_estimate=pl.CostEstimate(
                flops=cost * 2 * step * width * width,
                bytes_accessed=2 * step * width * 2,
                transcendentals=0,
            ),
            **options,
        )

    plan, pay1 = call(
        functools.partial(plan_kernel, tile_table.shape[0], bits, step),
        (array(8, dtype=jnp.int32), array(3 * step, width)),
        [SMEM_SPEC, HBM_SPEC],
        (SMEM_SPEC, HBM_SPEC),
        [pltpu.VMEM((3 * step, width), dtype), dma((3, 2))],
        mebi=61,
    )(tile_table, factors)
    got1 = swap(pay1, "orb", 0)

    def halves(pairs):
        kept = array(pairs, width // 2, width, dtype=jnp.float32)
        return kept, array(pairs, width // 2, width, dtype=wires[0])

    square = pltpu.VMEM((width, width), jnp.float32)

    def prepare():
        return call(
            functools.partial(weigh_kernel, step),
            (
                array(1, shard, width, dtype=jnp.float32),
                array(2, shard, width, dtype=jnp.float32),
                array(2 * step, width),
            ),
            [SMEM_SPEC, SMEM_SPEC, VMEM_SPEC, HBM_SPEC],
            (VMEM_SPEC, VMEM_SPEC, HBM_SPEC),
            [pltpu.VMEM((2 * step, width), dtype), dma((2, 2))],
        )(plan, occ_energy, virt_energy, factors)

    def own_chain():
        kept, sent = call(
            functools.partial(own_kernel, step),
            halves(1),
            [SMEM_SPEC, HBM_SPEC],
            (VMEM_SPEC, VMEM_SPEC),
            [pltpu.VMEM(factors.shape, dtype), square, dma((4,))],
            4,
        )(plan, factors)
        own_weight, weights, pay_a = prepare()
        sum01 = halve(kept, sent, "aux", wires)
        part01 = widen((sum01 * own_weight).astype(dtype)[None], "aux", reversed(range(2, bits)))
        return part01, weights, pay_a

    def no_chain():
        return jnp.zeros((aux // 4, 1, shard, width), dtype), *prepare()[1:]

    part01, weights, pay_a = lax.cond(plan[COUNTS] > 0, own_chain, no_chain)
    used = plan[COUNTS + 1] + plan[COUNTS + 2] > 0
    got1, part01, weights, pay_a, used = lax.optimization_barrier(
        (got1, part01, weights, pay_a, used)
    )
    got_a = swap(pay_a, "orb", 0)

    def pair_chain():
        kept, sent, pay_b = call(
            functools.partial(pair_kernel, step),
            (*halves(2), array(4 * unit, width)),
            [SMEM_SPEC, HBM_SPEC, HBM_SPEC],
            (VMEM_SPEC, VMEM_SPEC, HBM_SPEC),
            [
                pltpu.VMEM((3 * step, width), dtype),
                pltpu.VMEM((2 * step, width), dtype),
                pltpu.VMEM((3 * step, width), dtype),
                square,
                square,
                pltpu.VMEM((4 * unit, width), dtype),
                dma((8,)),
                dma((3, 2)),
            ],
            5,
        )(plan, factors, got1)
        return halve(kept, sent, "aux", wires), pay_b, *double(part01, "aux", 2)

    def no_pairs():
        pay_b = call(
            functools.partial(pack_kernel, unit),
            array(4 * unit, width),
            [SMEM_SPEC, HBM_SPEC],
            HBM_SPEC,
            [pltpu.VMEM((4 * unit, width), dtype), dma((3, 2))],
        )(plan, factors)
        return jnp.zeros((2, shard, width), jnp.float32), pay_b, *double(part01, "aux", 2)

    sums, pay_b, near01, far01 = lax.cond(used, pair_chain, no_pairs)
    sums, got_a, pay_b = lax.optimization_barrier((sums, got_a, pay_b))
    sums = sums + swap(sums.astype(WIRE), "orb", 0).astype(jnp.float32)
    shards0, pay_b = lax.optimization_barrier(((sums * weights).astype(dtype), pay_b))
    got_b = swap(pay_b, "orb", 0)

    def gather():
        return double(shards0[None], "aux", bits)

    def nothing():
        half = jnp.zeros((aux // 2, 2, shard, width), dtype)
        return half, half

    near, far = lax.cond(used, gather, nothing)

    def whole(shape):
        return pl.BlockSpec(shape, lambda i, plan: (0,) * len(shape))

    def run(kernel, steps, specs, out_shape, out_specs, scratch, cost, mebi=16):
        return pl.pallas_call(
            kernel,
            out_shape=out_shape,
            grid_spec=pltpu.PrefetchScalarGridSpec(
                num_scalar_prefetch=1,
                grid=(steps,),
                in_specs=specs,
                out_specs=out_specs,
                scratch_shapes=scratch,
            ),
            compiler_params=pltpu.CompilerParams(vmem_limit_bytes=mebi * MEBI),
            cost_estimate=pl.CostEstimate(
                flops=cost * 2 * step * width * width,
                bytes_accessed=cost * step * width * 2,
                transcendentals=0,
            ),
        )

    amp = pltpu.VMEM((width, width), dtype)
    back = run(
        back_kernel,
        1,
        [
            whole(near.shape),
            whole(far.shape),
            pl.BlockSpec((2, unit, width), lambda i, plan: (0, 0, 0)),
        ],
        array(unit, width),
        whole((unit, width)),
        [amp, amp],
        1,
    )(plan, near, far, factors)
    got_back = swap(back, "orb", 0)

    gamma = call(
        functools.partial(last_kernel, step),
        array(*factors.shape),
        [SMEM_SPEC] + [HBM_SPEC] * 8,
        HBM_SPEC,
        [
            pltpu.VMEM((2, *near01.shape), dtype),
            pltpu.VMEM((2, *near.shape), dtype),
            pltpu.VMEM((14 * unit, width), dtype),
            pltpu.VMEM(factors.shape, dtype),
            pltpu.VMEM(factors.shape, dtype),
            pltpu.VMEM((3, width, width), dtype),
            dma((12,)),
            dma((5,)),
        ],
        12,
        mebi=32,
    )(plan, near01, far01, near, far, got1, got_a, got_b, factors)
    return call(
        functools.partial(put_kernel, unit),
        array(*factors.shape),
        [SMEM_SPEC, VMEM_SPEC, HBM_SPEC],
        HBM_SPEC,
        [dma],
        input_output_aliases={2: 0},
    )(plan, got_back, gamma)


def shards(factors, occ_energy, virt_energy, tile_table):
    groups = lax.axis_size("orb")
    aux = lax.axis_size("aux")
    simple = groups == 2 and factors.shape[0] == 2 and tile_table.shape[0] <= CAP
    width = factors.shape[2]
    whole_shards = aux >= 4 and aux & (aux - 1) == 0 and width % (32 * aux) == 0
    if simple and whole_shards and factors.shape[1] % 128 == 0:
        return two_groups(factors, occ_energy, virt_energy, tile_table)
    return general(factors, occ_energy, virt_energy, tile_table)


def solution(mesh):
    return jax.shard_map(
        shards,
        mesh=mesh,
        in_specs=(P("orb", "aux", None), P(), P(), P()),
        out_specs=P("orb", "aux", None),
        check_vma=False,
    )
```

```python
import functools

import jax
import jax.numpy as jnp
from jax import lax
from jax.experimental import pallas as pl
from jax.experimental.pallas import tpu as pltpu
from jax.sharding import PartitionSpec as P

CAP = 4
WIRE = jnp.bfloat16
HELPS, FOREIGN, PLACE, COUNTS, LOW, PARTNER = 0, 1, 2, 3, 6, 7
MEBI = 1024 * 1024
SMEM_SPEC = pl.BlockSpec(memory_space=pltpu.SMEM)
HBM_SPEC = pl.BlockSpec(memory_space=pltpu.HBM)
VMEM_SPEC = pl.BlockSpec(memory_space=pltpu.VMEM)


def general(factors, occ_energy, virt_energy, tile_table):
    owned = factors.shape[0]
    width = factors.shape[2]
    tiles = tile_table.shape[0]
    groups = lax.axis_size("orb")
    mine = lax.axis_index("orb")
    first = tile_table[:, 0]
    second = tile_table[:, 1]
    helper = tile_table[:, 2]
    block_ids = jnp.arange(owned * groups, dtype=jnp.int32)
    group_ids = jnp.arange(groups, dtype=jnp.int32)
    local_ids = jnp.arange(owned, dtype=jnp.int32)
    touched = (
        (first[:, None] == block_ids[None, :]) | (second[:, None] == block_ids[None, :])
    ).astype(jnp.int32)
    helped = (helper[:, None] == group_ids[None, :]).astype(jnp.int32)
    usage = jnp.sum(helped[:, :, None] * touched[:, None, :], axis=0) > 0
    usage = usage.reshape(groups, groups, owned).astype(jnp.int32)
    own_usage = jnp.take(usage, mine, axis=1)
    send_pick = jnp.sum(own_usage * local_ids[None, :], axis=1)
    outgoing = jnp.stack(
        [
            lax.dynamic_index_in_dim(factors, send_pick[group], 0, keepdims=False)
            for group in range(groups)
        ]
    )
    incoming = lax.all_to_all(outgoing, "orb", split_axis=0, concat_axis=0, tiled=True)
    store = jnp.concatenate([factors, incoming], axis=0)

    def position(block):
        owner = block // owned
        return jnp.where(owner == mine, block % owned, owned + owner)

    is_mine = (helper == mine).astype(jnp.int32)
    tile_ids = jnp.arange(tiles, dtype=jnp.int32)
    earlier = (tile_ids[None, :] < tile_ids[:, None]).astype(jnp.int32)
    rank = jnp.sum(earlier * is_mine[None, :], axis=1)
    slot_ids = jnp.arange(CAP, dtype=jnp.int32)
    picked = is_mine[None, :] * (rank[None, :] == slot_ids[:, None]).astype(jnp.int32)
    valid = jnp.sum(picked, axis=1)
    tile_p = jnp.sum(picked * first[None, :], axis=1)
    tile_q = jnp.sum(picked * second[None, :], axis=1)
    place_p = position(tile_p)
    place_q = position(tile_q)
    energy_p = jnp.take(virt_energy, tile_p, axis=0)
    energy_q = jnp.take(virt_energy, tile_q, axis=0)
    occ_sum = jnp.take(occ_energy, tile_p) + jnp.take(occ_energy, tile_q)
    denominators = energy_p[:, :, None] + energy_q[:, None, :] - occ_sum[:, None, None]

    def partners(slot):
        block_p = lax.dynamic_index_in_dim(store, place_p[slot], 0, keepdims=False)
        block_q = lax.dynamic_index_in_dim(store, place_q[slot], 0, keepdims=False)
        return (block_p, block_q)

    def fill(slot, buffer):
        block_p, block_q = partners(slot)
        return lax.dynamic_update_index_in_dim(buffer, outer(block_p, block_q), slot, 0)

    buffer = lax.fori_loop(0, CAP, fill, jnp.zeros((CAP, width, width), jnp.float32))
    summed = lax.psum(buffer, "aux")
    all_amps = (summed / denominators).astype(jnp.bfloat16)

    def apply_all(slot, gathered):
        block_p, block_q = partners(slot)
        amplitudes = lax.dynamic_index_in_dim(all_amps, slot, 0, keepdims=False)
        amplitudes = jnp.where(valid[slot] > 0, amplitudes, jnp.zeros_like(amplitudes))
        gathered = gathered.at[place_p[slot]].add(right_t(block_q, amplitudes))
        return gathered.at[place_q[slot]].add(right(block_p, amplitudes))

    gathered = lax.fori_loop(0, CAP, apply_all, jnp.zeros(store.shape, jnp.float32))
    helper_part = gathered[owned:].astype(jnp.bfloat16)
    returned = lax.all_to_all(helper_part, "orb", split_axis=0, concat_axis=0, tiled=True)
    landing = (send_pick[:, None] == local_ids[None, :]).astype(jnp.float32)
    gamma = gathered[:owned] + jnp.einsum(
        "dj,dav->jav", landing, returned.astype(jnp.float32), precision=lax.Precision.HIGHEST
    )
    return gamma.astype(jnp.bfloat16)


def outer(a, b):
    return lax.dot_general(a, b, (((0,), (0,)), ((), ())), preferred_element_type=jnp.float32)


def right(a, m):
    return jnp.dot(a, m, preferred_element_type=jnp.float32)


def right_t(a, m):
    return lax.dot_general(a, m, (((1,), (1,)), ((), ())), preferred_element_type=jnp.float32)


def swap(value, axis, bit):
    size = lax.axis_size(axis)
    return lax.ppermute(value, axis, [(i, i ^ (1 << bit)) for i in range(size)])


def direct(value, bits, e):
    mask = sum(1 << (bits - 1 - n) for n in range(bits - 1) if (e >> n) & 1)
    size = 1 << bits
    return lax.ppermute(value, "aux", [(i, i ^ mask) for i in range(size)])


def gather(part, bits):
    near = jnp.concatenate([part, direct(part, bits, 1 << (bits - 2))], axis=0)
    return near, swap(near, "aux", 0)


def gather_lower(part, bits):
    upper = 1 << (bits - 2)
    pieces = [part[None]] + [direct(part, bits, e)[None] for e in range(1, upper)]
    while len(pieces) > 1:
        pieces = [jnp.concatenate(pieces[n : n + 2], axis=0) for n in range(0, len(pieces), 2)]
    return pieces[0]


def join_kernel(shift, plan, kept, came, own, *others):
    _, size, _ = own.shape
    count = 1 + len(others)
    place = (plan[PLACE] >> shift) & (count - 1)
    for e, out in enumerate((own, *others)):
        rows = pl.ds(pl.multiple_of((place ^ e) * size, size), size)
        total = kept[:, rows, :] + came[:, rows, :].astype(jnp.float32)
        out[...] = total.astype(out.dtype)


def after(value, *others):
    return lax.optimization_barrier((value, *others))[0]


def start_all(copies):
    for copy in copies:
        copy.start()


def wait_all(copies):
    for copy in copies:
        copy.wait()


def staged(source, stage, target, sems):
    first = pltpu.make_async_copy(source, stage, sems.at[0])
    return first, pltpu.make_async_copy(stage, target, sems.at[1])


def relay(copies):
    for first, second in copies:
        first.wait()
        second.start()


def rows_at(unit, start, size):
    return pl.ds(pl.multiple_of(start * unit, unit), size * unit)


def plan_kernel(tiles, bits, step, table, factors, plan, pay, stage, sems):
    helper = table[0, 2]
    helps = (lax.axis_index("orb") == helper).astype(jnp.int32)
    low, foreign_low = helper * 2, (1 - helper) * 2
    foreign = jnp.int32(0)
    for t in range(tiles):
        named = (table[t, 0] == foreign_low + 1) | (table[t, 1] == foreign_low + 1)
        foreign = foreign | named.astype(jnp.int32)
    b0, b1 = jnp.where(helps == 1, 0, foreign), jnp.where(helps == 1, 1, foreign)
    sources = ((b0, 2 * helps), (b0, 2 * helps + 1), (b1, 2 + helps))
    copies = [
        staged(
            factors.at[block, rows_at(step, start, 1)],
            stage.at[pl.ds(n * step, step)],
            pay.at[pl.ds(n * step, step)],
            sems.at[n],
        )
        for n, (block, start) in enumerate(sources)
    ]
    start_all(first for first, _ in copies)
    me = lax.axis_index("aux")
    place = jnp.int32(0)
    for bit in range(bits):
        place = place * 2 + ((me >> bit) & 1)
    plan[HELPS], plan[FOREIGN], plan[PLACE] = helps, foreign, place
    plan[LOW], plan[PARTNER] = low, foreign_low + foreign
    pairs = ((low, low + 1), (low, foreign_low + foreign), (low + 1, foreign_low + foreign))
    for n, (a, b) in enumerate(pairs):
        count = jnp.int32(0)
        for t in range(tiles):
            p, q = table[t, 0], table[t, 1]
            same = ((p == a) & (q == b)) | ((p == b) & (q == a))
            count = count + same.astype(jnp.int32)
        plan[COUNTS + n] = count
    relay(copies)
    wait_all(second for _, second in copies)


def weigh_kernel(step, plan, occ, virt, factors, own_weight, weights, pay_a, stage, sems):
    helps, foreign = plan[HELPS], plan[FOREIGN]
    b0, b1 = jnp.where(helps == 1, 0, foreign), jnp.where(helps == 1, 1, foreign)
    copies = [
        staged(
            factors.at[block, rows_at(step, start, 1)],
            stage.at[pl.ds(n * step, step)],
            pay_a.at[pl.ds(n * step, step)],
            sems.at[n],
        )
        for n, (block, start) in enumerate(((b1, 3 - helps), (b0, 1)))
    ]
    start_all(first for first, _ in copies)
    low, partner = plan[LOW], plan[PARTNER]
    _, shard, width = own_weight.shape
    row = lax.broadcasted_iota(jnp.int32, (shard, width), 0)
    column = lax.broadcasted_iota(jnp.int32, (shard, width), 1)
    mine = column == row + plan[PLACE] * shard
    pairs = ((low, low + 1, own_weight, 0), (low, partner, weights, 0), (low + 1, partner, weights, 1))
    for n, (a, b, out, slot) in enumerate(pairs):
        virt_a = jnp.sum(jnp.where(mine, virt[pl.ds(a, 1), :], 0.0), axis=1, keepdims=True)
        denominators = virt_a + virt[pl.ds(b, 1), :] - occ[a] - occ[b]
        out[slot] = plan[COUNTS + n].astype(jnp.float32) / denominators
    relay(copies)
    wait_all(second for _, second in copies)


def third_rows(unit, plan, factors, pay_b, stage, sems):
    helps, foreign = plan[HELPS], plan[FOREIGN]
    b0, b1 = jnp.where(helps == 1, 0, foreign), jnp.where(helps == 1, 1, foreign)
    return [
        staged(
            factors.at[block, pl.ds(start * unit, size * unit)],
            stage.at[pl.ds(to * unit, size * unit)],
            pay_b.at[pl.ds(to * unit, size * unit)],
            sems.at[n],
        )
        for n, (block, start, size, to) in enumerate(((b1, 2, 2, 0), (b0, 1, 1, 2), (b1, 1, 1, 3)))
    ]


def pack_kernel(unit, plan, factors, pay_b, stage, sems):
    copies = third_rows(unit, plan, factors, pay_b, stage, sems)
    start_all(first for first, _ in copies)
    relay(copies)
    wait_all(second for _, second in copies)


def split_halves(acc, pair, kept, sent, core):
    half = kept.shape[1]
    kept[pair] = acc[pl.ds(pl.multiple_of(core * half, half), half), :]
    other = acc[pl.ds(pl.multiple_of((1 - core) * half, half), half), :]
    sent[pair] = other.astype(sent.dtype)


def own_kernel(step, plan, factors, kept, sent, rows, acc, sems):
    del plan
    copies = [
        pltpu.make_async_copy(
            factors.at[:, pl.ds(n * step, step)], rows.at[:, pl.ds(n * step, step)], sems.at[n]
        )
        for n in range(4)
    ]
    start_all(copies)
    for n in range(4):
        copies[n].wait()
        term = outer(rows[0, n * step : (n + 1) * step], rows[1, n * step : (n + 1) * step])
        acc[...] = term if n == 0 else acc[...] + term
    split_halves(acc, 0, kept, sent, lax.axis_index("aux") & 1)


def pair_kernel(
    step, plan, factors, got_hbm, kept, sent, pay_b, got, rows0, rows1, acc0, acc1, stage, sems, pay_sems
):
    helps, foreign = plan[HELPS], plan[FOREIGN]
    b0, b1 = jnp.where(helps == 1, 0, foreign), jnp.where(helps == 1, 1, foreign)

    def cut(ref, n):
        return ref[n * step : (n + 1) * step]

    def fetch(source, ref, n, slot):
        return pltpu.make_async_copy(source, ref.at[pl.ds(n * step, step)], sems.at[slot])

    gots = [fetch(got_hbm.at[pl.ds(n * step, step)], got, n, n) for n in range(3)]
    copies0 = [
        fetch(factors.at[b0, rows_at(step, jnp.where(helps == 1, n, 2 + n), 1)], rows0, n, 3 + n)
        for n in range(2)
    ]
    copies1 = [
        fetch(factors.at[b1, rows_at(step, jnp.where(helps == 1, n, 3), 1)], rows1, n, 5 + n)
        for n in range(3)
    ]
    start_all((gots[0], copies0[0], gots[1], copies0[1], gots[2], copies1[2], *copies1[:2]))
    pays = third_rows(step // 2, plan, factors, pay_b, stage, pay_sems)
    start_all(first for first, _ in pays)

    for n in range(2):
        wait_all((gots[n], copies0[n]))

        @pl.when(helps == 1)
        def _():
            term = outer(cut(rows0, n), cut(got, n))
            acc0[...] = term if n == 0 else acc0[...] + term

        @pl.when(helps == 0)
        def _():
            term = outer(cut(got, n), cut(rows0, n))
            acc0[...] = term if n == 0 else acc0[...] + term

    wait_all((gots[2], copies1[2]))

    @pl.when(helps == 1)
    def _():
        acc1[...] = outer(cut(rows1, 2), cut(got, 2))

    @pl.when(helps == 0)
    def _():
        acc1[...] = outer(cut(got, 2), cut(rows1, 2))

    wait_all(copies1[:2])
    relay(pays)

    @pl.when(helps == 1)
    def _():
        acc1[...] += outer(cut(rows1, 0), cut(got, 0)) + outer(cut(rows1, 1), cut(got, 1))

    core = lax.axis_index("aux") & 1
    split_halves(acc0, 0, kept, sent, core)
    split_halves(acc1, 1, kept, sent, core)
    wait_all(second for _, second in pays)


def arrange(plan, near, far, pair, out):
    count, _, shard, _ = near.shape
    for source, base in ((near, 0), (far, count)):
        for n in range(count):
            row = pl.multiple_of((plan[PLACE] ^ (base + n)) * shard, shard)
            out[pl.ds(row, shard), :] = source[n, pair]


def back_kernel(plan, near_hbm, far_hbm, factors, back, amp0, amp1, wide, rows, sems):
    unit = back.shape[0]
    copies = [
        pltpu.make_async_copy(near_hbm, wide.at[0], sems.at[0]),
        pltpu.make_async_copy(far_hbm, wide.at[1], sems.at[1]),
        pltpu.make_async_copy(factors.at[:, pl.ds(0, unit)], rows, sems.at[2]),
    ]
    start_all(copies)
    wait_all(copies)
    arrange(plan, wide.at[0], wide.at[1], 0, amp0)
    arrange(plan, wide.at[0], wide.at[1], 1, amp1)
    total = right(rows[0], amp0[...]) + right(rows[1], amp1[...])
    back[...] = total.astype(back.dtype)


def last_kernel(
    step, plan, near01, far01, amp0, amp1, got1, got_a, got_b, factors, gamma, small, rows, own, out, own_amp, ins, outs
):
    unit = step // 2
    foreign = plan[FOREIGN]

    def part(start, size):
        return pl.ds(start * unit, size * unit)

    def copy(source, target, slot):
        return pltpu.make_async_copy(source, target, ins.at[slot])

    @pl.when(plan[HELPS] == 1)
    def _():
        singles = [copy(near01, small.at[0], 2), copy(far01, small.at[1], 3)]
        sources = [got1.at[part(2 * n, 2)] for n in range(3)] + [got_a.at[part(0, 2)]]
        others = [copy(sources[n], rows.at[part(2 * n, 2)], 4 + n) for n in range(4)]
        mine = [copy(factors.at[:, part(2 * n, 2)], own.at[:, part(2 * n, 2)], 8 + n) for n in range(4)]
        start_all(singles)
        for n in range(4):
            start_all((mine[n], others[n]))
        wait_all(singles)
        arrange(plan, small.at[0], small.at[1], 0, own_amp)
        results = []
        for n in range(4):
            wait_all((mine[n], others[n]))
            at = slice(n * step, (n + 1) * step)
            first = right_t(own[1, at], own_amp[...]) + right_t(rows[at], amp0[...])
            out[0, at] = first.astype(out.dtype)
            second = right(own[0, at], own_amp[...]) + right_t(rows[at], amp1[...])
            out[1, at] = second.astype(out.dtype)
            place = part(2 * n, 2)
            results.append(pltpu.make_async_copy(out.at[:, place], gamma.at[:, place], outs.at[n]))
            results[-1].start()
        wait_all(results)

    @pl.when(plan[HELPS] == 0)
    def _():
        others = [
            copy(got1, rows.at[part(0, 6)], 4),
            copy(got_a, rows.at[part(6, 4)], 5),
            copy(got_b, rows.at[part(10, 4)], 6),
        ]
        start_all(others)
        out[0] = jnp.zeros_like(out[0])
        results = [pltpu.make_async_copy(out.at[0], gamma.at[1 - foreign], outs.at[0])]
        results[0].start()
        wait_all(others)
        pieces = ((6, 2, 2, 4), (4, 2, 0, 6), (2, 2, 8, 10), (1, 1, 12, 13))
        for n, (start, size, row0, row1) in enumerate(pieces):
            rows0 = rows[row0 * unit : (row0 + size) * unit]
            rows1 = rows[row1 * unit : (row1 + size) * unit]
            total = right(rows0, amp0[...]) + right(rows1, amp1[...])
            out[1, start * unit : (start + size) * unit] = total.astype(out.dtype)
            place = part(start, size)
            results.append(
                pltpu.make_async_copy(out.at[1, place], gamma.at[foreign, place], outs.at[1 + n])
            )
            results[-1].start()
        wait_all(results)


def put_kernel(unit, plan, back, gamma_in, gamma, sem):
    @pl.when(plan[HELPS] == 0)
    def _():
        copy = pltpu.make_async_copy(back, gamma.at[plan[FOREIGN], pl.ds(0, unit)], sem)
        copy.start()
        copy.wait()


def two_groups(factors, occ_energy, virt_energy, tile_table):
    owned, rows, width = factors.shape
    aux = lax.axis_size("aux")
    bits = aux.bit_length() - 1
    step, unit = rows // 4, rows // 8
    shard = width // aux
    dtype = factors.dtype
    dma = pltpu.SemaphoreType.DMA

    def array(*shape, dtype=dtype):
        return jax.ShapeDtypeStruct(shape, dtype)

    def call(kernel, out_shape, in_specs, out_specs, scratch, cost=0, mebi=16, **options):
        return pl.pallas_call(
            kernel,
            out_shape=out_shape,
            in_specs=in_specs,
            out_specs=out_specs,
            scratch_shapes=scratch,
            compiler_params=pltpu.CompilerParams(vmem_limit_bytes=mebi * MEBI),
            cost_estimate=pl.CostEstimate(
                flops=cost * 2 * step * width * width,
                bytes_accessed=2 * step * width * 2,
                transcendentals=0,
            ),
            **options,
        )

    plan, pay1 = call(
        functools.partial(plan_kernel, tile_table.shape[0], bits, step),
        (array(8, dtype=jnp.int32), array(3 * step, width)),
        [SMEM_SPEC, HBM_SPEC],
        (SMEM_SPEC, HBM_SPEC),
        [pltpu.VMEM((3 * step, width), dtype), dma((3, 2))],
        mebi=61,
    )(tile_table, factors)
    got1 = swap(pay1, "orb", 0)

    def halves(pairs):
        kept = array(pairs, width // 2, width, dtype=jnp.float32)
        return kept, array(pairs, width // 2, width, dtype=WIRE)

    square = pltpu.VMEM((width, width), jnp.float32)

    def scatter(kept, sent):
        upper = aux // 4

        def join(kept, came, shift, count):
            shape = (kept.shape[0], kept.shape[1] // count, width)
            return call(
                functools.partial(join_kernel, shift),
                (array(*shape, dtype=jnp.float32), *[array(*shape, dtype=WIRE)] * (count - 1)),
                [SMEM_SPEC, VMEM_SPEC, VMEM_SPEC],
                (VMEM_SPEC,) * count,
                [],
            )(plan, kept, came)

        kept, sent = join(kept, swap(sent, "aux", 0), bits - 2, 2)
        own, *sends = join(kept, direct(sent, bits, upper), 0, upper)
        for term in [direct(send, bits, 1 + n) for n, send in enumerate(sends)]:
            own = own + term.astype(jnp.float32)
        return own

    def prepare():
        return call(
            functools.partial(weigh_kernel, step),
            (
                array(1, shard, width, dtype=jnp.float32),
                array(2, shard, width, dtype=jnp.float32),
                array(2 * step, width),
            ),
            [SMEM_SPEC, SMEM_SPEC, VMEM_SPEC, HBM_SPEC],
            (VMEM_SPEC, VMEM_SPEC, HBM_SPEC),
            [pltpu.VMEM((2 * step, width), dtype), dma((2, 2))],
        )(plan, occ_energy, virt_energy, factors)

    def own_chain():
        kept, sent = call(
            functools.partial(own_kernel, step),
            halves(1),
            [SMEM_SPEC, HBM_SPEC],
            (VMEM_SPEC, VMEM_SPEC),
            [pltpu.VMEM(factors.shape, dtype), square, dma((4,))],
            4,
        )(plan, factors)
        own_weight, weights, pay_a = prepare()
        shards01 = (scatter(kept, sent) * own_weight).astype(dtype)
        return gather_lower(shards01, bits), weights, pay_a

    def no_chain():
        return jnp.zeros((aux // 4, 1, shard, width), dtype), *prepare()[1:]

    part01, weights, pay_a = lax.cond(plan[COUNTS] > 0, own_chain, no_chain)
    used = plan[COUNTS + 1] + plan[COUNTS + 2] > 0
    got1, part01, weights, pay_a, used = lax.optimization_barrier(
        (got1, part01, weights, pay_a, used)
    )
    got_a = swap(pay_a, "orb", 0)

    def pair_chain():
        kept, sent, pay_b = call(
            functools.partial(pair_kernel, step),
            (*halves(2), array(4 * unit, width)),
            [SMEM_SPEC, HBM_SPEC, HBM_SPEC],
            (VMEM_SPEC, VMEM_SPEC, HBM_SPEC),
            [
                pltpu.VMEM((3 * step, width), dtype),
                pltpu.VMEM((2 * step, width), dtype),
                pltpu.VMEM((3 * step, width), dtype),
                square,
                square,
                pltpu.VMEM((4 * unit, width), dtype),
                dma((8,)),
                dma((3, 2)),
            ],
            5,
        )(plan, factors, got1)
        return scatter(kept, sent), pay_b, *gather(part01, bits)

    def no_pairs():
        pay_b = call(
            functools.partial(pack_kernel, unit),
            array(4 * unit, width),
            [SMEM_SPEC, HBM_SPEC],
            HBM_SPEC,
            [pltpu.VMEM((4 * unit, width), dtype), dma((3, 2))],
        )(plan, factors)
        return jnp.zeros((2, shard, width), jnp.float32), pay_b, *gather(part01, bits)

    sums, pay_b, near01, far01 = lax.cond(used, pair_chain, no_pairs)
    sums, got_a, pay_b = lax.optimization_barrier((sums, got_a, pay_b))
    sums = sums + swap(sums.astype(WIRE), "orb", 0).astype(jnp.float32)
    shards0, pay_b = lax.optimization_barrier(((sums * weights).astype(dtype), pay_b))
    got_b = swap(pay_b, "orb", 0)

    def nothing():
        half = jnp.zeros((aux // 2, 2, shard, width), dtype)
        return half, half

    near, far = lax.cond(used, lambda: gather(gather_lower(shards0, bits), bits), nothing)

    amp = array(width, width)
    back, amp0, amp1 = call(
        back_kernel,
        (array(unit, width), amp, amp),
        [SMEM_SPEC] + [HBM_SPEC] * 3,
        (VMEM_SPEC,) * 3,
        [
            pltpu.VMEM((2, *near.shape), dtype),
            pltpu.VMEM((2, unit, width), dtype),
            dma((3,)),
        ],
        1,
    )(plan, near, far, factors)
    got_back = swap(back, "orb", 0)

    gamma = call(
        functools.partial(last_kernel, step),
        array(*factors.shape),
        [SMEM_SPEC] + [HBM_SPEC] * 2 + [VMEM_SPEC] * 2 + [HBM_SPEC] * 4,
        HBM_SPEC,
        [
            pltpu.VMEM((2, *near01.shape), dtype),
            pltpu.VMEM((14 * unit, width), dtype),
            pltpu.VMEM(factors.shape, dtype),
            pltpu.VMEM(factors.shape, dtype),
            pltpu.VMEM((width, width), dtype),
            dma((12,)),
            dma((5,)),
        ],
        12,
        mebi=32,
    )(plan, near01, far01, amp0, amp1, got1, got_a, got_b, factors)
    return call(
        functools.partial(put_kernel, unit),
        array(*factors.shape),
        [SMEM_SPEC, VMEM_SPEC, HBM_SPEC],
        HBM_SPEC,
        [dma],
        input_output_aliases={2: 0},
    )(plan, got_back, gamma)


def shards(factors, occ_energy, virt_energy, tile_table):
    groups = lax.axis_size("orb")
    aux = lax.axis_size("aux")
    simple = groups == 2 and factors.shape[0] == 2 and tile_table.shape[0] <= CAP
    width = factors.shape[2]
    whole_shards = aux >= 4 and aux & (aux - 1) == 0 and width % (32 * aux) == 0
    if simple and whole_shards and factors.shape[1] % 128 == 0:
        return two_groups(factors, occ_energy, virt_energy, tile_table)
    return general(factors, occ_energy, virt_energy, tile_table)


def solution(mesh):
    return jax.shard_map(
        shards,
        mesh=mesh,
        in_specs=(P("orb", "aux", None), P(), P(), P()),
        out_specs=P("orb", "aux", None),
        check_vma=False,
    )
```

```python
import functools

import jax
import jax.numpy as jnp
from jax import lax
from jax.experimental import pallas as pl
from jax.experimental.pallas import tpu as pltpu
from jax.sharding import PartitionSpec as P

CAP = 4
WIRE = jnp.bfloat16
HELPS, FOREIGN, PLACE, COUNTS, LOW, PARTNER = 0, 1, 2, 3, 6, 7
MEBI = 1024 * 1024
SMEM_SPEC = pl.BlockSpec(memory_space=pltpu.SMEM)
HBM_SPEC = pl.BlockSpec(memory_space=pltpu.HBM)
VMEM_SPEC = pl.BlockSpec(memory_space=pltpu.VMEM)


def general(factors, occ_energy, virt_energy, tile_table):
    owned = factors.shape[0]
    width = factors.shape[2]
    tiles = tile_table.shape[0]
    groups = lax.axis_size("orb")
    mine = lax.axis_index("orb")
    first = tile_table[:, 0]
    second = tile_table[:, 1]
    helper = tile_table[:, 2]
    block_ids = jnp.arange(owned * groups, dtype=jnp.int32)
    group_ids = jnp.arange(groups, dtype=jnp.int32)
    local_ids = jnp.arange(owned, dtype=jnp.int32)
    touched = (
        (first[:, None] == block_ids[None, :]) | (second[:, None] == block_ids[None, :])
    ).astype(jnp.int32)
    helped = (helper[:, None] == group_ids[None, :]).astype(jnp.int32)
    usage = jnp.sum(helped[:, :, None] * touched[:, None, :], axis=0) > 0
    usage = usage.reshape(groups, groups, owned).astype(jnp.int32)
    own_usage = jnp.take(usage, mine, axis=1)
    send_pick = jnp.sum(own_usage * local_ids[None, :], axis=1)
    outgoing = jnp.stack(
        [
            lax.dynamic_index_in_dim(factors, send_pick[group], 0, keepdims=False)
            for group in range(groups)
        ]
    )
    incoming = lax.all_to_all(outgoing, "orb", split_axis=0, concat_axis=0, tiled=True)
    store = jnp.concatenate([factors, incoming], axis=0)

    def position(block):
        owner = block // owned
        return jnp.where(owner == mine, block % owned, owned + owner)

    is_mine = (helper == mine).astype(jnp.int32)
    tile_ids = jnp.arange(tiles, dtype=jnp.int32)
    earlier = (tile_ids[None, :] < tile_ids[:, None]).astype(jnp.int32)
    rank = jnp.sum(earlier * is_mine[None, :], axis=1)
    slot_ids = jnp.arange(CAP, dtype=jnp.int32)
    picked = is_mine[None, :] * (rank[None, :] == slot_ids[:, None]).astype(jnp.int32)
    valid = jnp.sum(picked, axis=1)
    tile_p = jnp.sum(picked * first[None, :], axis=1)
    tile_q = jnp.sum(picked * second[None, :], axis=1)
    place_p = position(tile_p)
    place_q = position(tile_q)
    energy_p = jnp.take(virt_energy, tile_p, axis=0)
    energy_q = jnp.take(virt_energy, tile_q, axis=0)
    occ_sum = jnp.take(occ_energy, tile_p) + jnp.take(occ_energy, tile_q)
    denominators = energy_p[:, :, None] + energy_q[:, None, :] - occ_sum[:, None, None]

    def partners(slot):
        block_p = lax.dynamic_index_in_dim(store, place_p[slot], 0, keepdims=False)
        block_q = lax.dynamic_index_in_dim(store, place_q[slot], 0, keepdims=False)
        return (block_p, block_q)

    def fill(slot, buffer):
        block_p, block_q = partners(slot)
        return lax.dynamic_update_index_in_dim(buffer, outer(block_p, block_q), slot, 0)

    buffer = lax.fori_loop(0, CAP, fill, jnp.zeros((CAP, width, width), jnp.float32))
    summed = lax.psum(buffer, "aux")
    all_amps = (summed / denominators).astype(jnp.bfloat16)

    def apply_all(slot, gathered):
        block_p, block_q = partners(slot)
        amplitudes = lax.dynamic_index_in_dim(all_amps, slot, 0, keepdims=False)
        amplitudes = jnp.where(valid[slot] > 0, amplitudes, jnp.zeros_like(amplitudes))
        gathered = gathered.at[place_p[slot]].add(right_t(block_q, amplitudes))
        return gathered.at[place_q[slot]].add(right(block_p, amplitudes))

    gathered = lax.fori_loop(0, CAP, apply_all, jnp.zeros(store.shape, jnp.float32))
    helper_part = gathered[owned:].astype(jnp.bfloat16)
    returned = lax.all_to_all(helper_part, "orb", split_axis=0, concat_axis=0, tiled=True)
    landing = (send_pick[:, None] == local_ids[None, :]).astype(jnp.float32)
    gamma = gathered[:owned] + jnp.einsum(
        "dj,dav->jav", landing, returned.astype(jnp.float32), precision=lax.Precision.HIGHEST
    )
    return gamma.astype(jnp.bfloat16)


def outer(a, b):
    return lax.dot_general(a, b, (((0,), (0,)), ((), ())), preferred_element_type=jnp.float32)


def right(a, m):
    return jnp.dot(a, m, preferred_element_type=jnp.float32)


def right_t(a, m):
    return lax.dot_general(a, m, (((1,), (1,)), ((), ())), preferred_element_type=jnp.float32)


def swap(value, axis, bit):
    size = lax.axis_size(axis)
    return lax.ppermute(value, axis, [(i, i ^ (1 << bit)) for i in range(size)])


def direct(value, bits, e):
    mask = sum(1 << (bits - 1 - n) for n in range(bits - 1) if (e >> n) & 1)
    size = 1 << bits
    return lax.ppermute(value, "aux", [(i, i ^ mask) for i in range(size)])


def gather(part, bits):
    near = jnp.concatenate([part, direct(part, bits, 1 << (bits - 2))], axis=0)
    return near, swap(near, "aux", 0)


def gather_lower(part, bits):
    upper = 1 << (bits - 2)
    pieces = [part[None]] + [direct(part, bits, e)[None] for e in range(1, upper)]
    while len(pieces) > 1:
        pieces = [jnp.concatenate(pieces[n : n + 2], axis=0) for n in range(0, len(pieces), 2)]
    return pieces[0]


def join_kernel(shift, plan, kept, came, own, *others):
    _, size, _ = own.shape
    count = 1 + len(others)
    place = (plan[PLACE] >> shift) & (count - 1)
    for e, out in enumerate((own, *others)):
        rows = pl.ds(pl.multiple_of((place ^ e) * size, size), size)
        total = kept[:, rows, :] + came[:, rows, :].astype(jnp.float32)
        out[...] = total.astype(out.dtype)


def after(value, *others):
    return lax.optimization_barrier((value, *others))[0]


def start_all(copies):
    for copy in copies:
        copy.start()


def wait_all(copies):
    for copy in copies:
        copy.wait()


def staged(source, stage, target, sems):
    first = pltpu.make_async_copy(source, stage, sems.at[0])
    return first, pltpu.make_async_copy(stage, target, sems.at[1])


def relay(copies):
    for first, second in copies:
        first.wait()
        second.start()


def rows_at(unit, start, size):
    return pl.ds(pl.multiple_of(start * unit, unit), size * unit)


def plan_kernel(tiles, bits, step, table, factors, plan, pay, stage, sems):
    helper = table[0, 2]
    helps = (lax.axis_index("orb") == helper).astype(jnp.int32)
    low, foreign_low = helper * 2, (1 - helper) * 2
    foreign = jnp.int32(0)
    for t in range(tiles):
        named = (table[t, 0] == foreign_low + 1) | (table[t, 1] == foreign_low + 1)
        foreign = foreign | named.astype(jnp.int32)
    b0, b1 = jnp.where(helps == 1, 0, foreign), jnp.where(helps == 1, 1, foreign)
    sources = ((b0, 2 * helps), (b0, 2 * helps + 1), (b1, 2 + helps))
    copies = [
        staged(
            factors.at[block, rows_at(step, start, 1)],
            stage.at[pl.ds(n * step, step)],
            pay.at[pl.ds(n * step, step)],
            sems.at[n],
        )
        for n, (block, start) in enumerate(sources)
    ]
    start_all(first for first, _ in copies)
    me = lax.axis_index("aux")
    place = jnp.int32(0)
    for bit in range(bits):
        place = place * 2 + ((me >> bit) & 1)
    plan[HELPS], plan[FOREIGN], plan[PLACE] = helps, foreign, place
    plan[LOW], plan[PARTNER] = low, foreign_low + foreign
    pairs = ((low, low + 1), (low, foreign_low + foreign), (low + 1, foreign_low + foreign))
    for n, (a, b) in enumerate(pairs):
        count = jnp.int32(0)
        for t in range(tiles):
            p, q = table[t, 0], table[t, 1]
            same = ((p == a) & (q == b)) | ((p == b) & (q == a))
            count = count + same.astype(jnp.int32)
        plan[COUNTS + n] = count
    relay(copies)
    wait_all(second for _, second in copies)


def weigh_kernel(step, plan, occ, virt, factors, own_weight, weights, pay_a, pay_b, stage, sems):
    piece = step // 4
    helps, foreign = plan[HELPS], plan[FOREIGN]
    b0, b1 = jnp.where(helps == 1, 0, foreign), jnp.where(helps == 1, 1, foreign)
    moves = (
        (b1, 12 - 4 * helps, 4, pay_a, 0, 0),
        (b0, 4, 4, pay_a, 4, 4),
        (b1, 7, 1, pay_a, 8, 8),
        (b1, 4, 3, pay_b, 0, 9),
        (b0, 2, 2, pay_b, 3, 12),
        (b1, 2, 2, pay_b, 5, 14),
    )
    copies = [
        staged(
            factors.at[block, rows_at(piece, start, size)],
            stage.at[pl.ds(between * piece, size * piece)],
            pay.at[pl.ds(to * piece, size * piece)],
            sems.at[n],
        )
        for n, (block, start, size, pay, to, between) in enumerate(moves)
    ]
    start_all(first for first, _ in copies)
    low, partner = plan[LOW], plan[PARTNER]
    _, shard, width = own_weight.shape
    row = lax.broadcasted_iota(jnp.int32, (shard, width), 0)
    column = lax.broadcasted_iota(jnp.int32, (shard, width), 1)
    mine = column == row + plan[PLACE] * shard
    pairs = ((low, low + 1, own_weight, 0), (low, partner, weights, 0), (low + 1, partner, weights, 1))
    for n, (a, b, out, slot) in enumerate(pairs):
        virt_a = jnp.sum(jnp.where(mine, virt[pl.ds(a, 1), :], 0.0), axis=1, keepdims=True)
        denominators = virt_a + virt[pl.ds(b, 1), :] - occ[a] - occ[b]
        out[slot] = plan[COUNTS + n].astype(jnp.float32) / denominators
    relay(copies)
    wait_all(second for _, second in copies)


def split_halves(acc, pair, kept, sent, core):
    half = kept.shape[1]
    kept[pair] = acc[pl.ds(pl.multiple_of(core * half, half), half), :]
    other = acc[pl.ds(pl.multiple_of((1 - core) * half, half), half), :]
    sent[pair] = other.astype(sent.dtype)


def own_kernel(step, plan, factors, kept, sent, rows, acc, sems):
    del plan
    copies = [
        pltpu.make_async_copy(
            factors.at[:, pl.ds(n * step, step)], rows.at[:, pl.ds(n * step, step)], sems.at[n]
        )
        for n in range(4)
    ]
    start_all(copies)
    for n in range(4):
        copies[n].wait()
        term = outer(rows[0, n * step : (n + 1) * step], rows[1, n * step : (n + 1) * step])
        acc[...] = term if n == 0 else acc[...] + term
    split_halves(acc, 0, kept, sent, lax.axis_index("aux") & 1)


def pair_kernel(
    step, plan, factors, got_hbm, kept, sent, got, rows0, rows1, acc0, acc1, sems
):
    helps, foreign = plan[HELPS], plan[FOREIGN]
    b0, b1 = jnp.where(helps == 1, 0, foreign), jnp.where(helps == 1, 1, foreign)

    def cut(ref, n):
        return ref[n * step : (n + 1) * step]

    def fetch(source, ref, n, slot):
        return pltpu.make_async_copy(source, ref.at[pl.ds(n * step, step)], sems.at[slot])

    gots = [fetch(got_hbm.at[pl.ds(n * step, step)], got, n, n) for n in range(3)]
    copies0 = [
        fetch(factors.at[b0, rows_at(step, jnp.where(helps == 1, n, 2 + n), 1)], rows0, n, 3 + n)
        for n in range(2)
    ]
    copies1 = [
        fetch(factors.at[b1, rows_at(step, jnp.where(helps == 1, n, 3), 1)], rows1, n, 5 + n)
        for n in range(3)
    ]
    start_all((gots[0], copies0[0], gots[1], copies0[1], gots[2], copies1[2], *copies1[:2]))

    for n in range(2):
        wait_all((gots[n], copies0[n]))

        @pl.when(helps == 1)
        def _():
            term = outer(cut(rows0, n), cut(got, n))
            acc0[...] = term if n == 0 else acc0[...] + term

        @pl.when(helps == 0)
        def _():
            term = outer(cut(got, n), cut(rows0, n))
            acc0[...] = term if n == 0 else acc0[...] + term

    wait_all((gots[2], copies1[2]))

    @pl.when(helps == 1)
    def _():
        acc1[...] = outer(cut(rows1, 2), cut(got, 2))

    @pl.when(helps == 0)
    def _():
        acc1[...] = outer(cut(got, 2), cut(rows1, 2))

    wait_all(copies1[:2])

    @pl.when(helps == 1)
    def _():
        acc1[...] += outer(cut(rows1, 0), cut(got, 0)) + outer(cut(rows1, 1), cut(got, 1))

    core = lax.axis_index("aux") & 1
    split_halves(acc0, 0, kept, sent, core)
    split_halves(acc1, 1, kept, sent, core)


def arrange(plan, near, far, pair, out):
    count, _, shard, _ = near.shape
    for source, base in ((near, 0), (far, count)):
        for n in range(count):
            row = pl.multiple_of((plan[PLACE] ^ (base + n)) * shard, shard)
            out[pl.ds(row, shard), :] = source[n, pair]


def back_kernel(plan, near, far, factors, back, amp0, amp1, rows, sem):
    copy = pltpu.make_async_copy(factors.at[:, pl.ds(0, back.shape[0])], rows, sem)
    copy.start()
    arrange(plan, near, far, 0, amp0)
    arrange(plan, near, far, 1, amp1)
    copy.wait()
    total = right(rows[0], amp0[...]) + right(rows[1], amp1[...])
    back[...] = total.astype(back.dtype)


def last_kernel(
    step, plan, near01, far01, amp0, amp1, got1, got_a, got_b, factors, gamma, small, rows, own, out, own_amp, ins, outs
):
    unit, piece = step // 2, step // 4
    foreign = plan[FOREIGN]

    def part(start, size):
        return pl.ds(start * unit, size * unit)

    def copy(source, target, slot):
        return pltpu.make_async_copy(source, target, ins.at[slot])

    @pl.when(plan[HELPS] == 1)
    def _():
        singles = [copy(near01, small.at[0], 2), copy(far01, small.at[1], 3)]
        sources = [got1.at[part(2 * n, 2)] for n in range(3)] + [got_a.at[part(0, 2)]]
        others = [copy(sources[n], rows.at[part(2 * n, 2)], 4 + n) for n in range(4)]
        mine = [copy(factors.at[:, part(2 * n, 2)], own.at[:, part(2 * n, 2)], 8 + n) for n in range(4)]
        start_all(singles)
        for n in range(4):
            start_all((mine[n], others[n]))
        wait_all(singles)
        arrange(plan, small.at[0], small.at[1], 0, own_amp)
        results = []
        for n in range(4):
            wait_all((mine[n], others[n]))
            at = slice(n * step, (n + 1) * step)
            first = right_t(own[1, at], own_amp[...]) + right_t(rows[at], amp0[...])
            out[0, at] = first.astype(out.dtype)
            second = right(own[0, at], own_amp[...]) + right_t(rows[at], amp1[...])
            out[1, at] = second.astype(out.dtype)
            place = part(2 * n, 2)
            results.append(pltpu.make_async_copy(out.at[:, place], gamma.at[:, place], outs.at[n]))
            results[-1].start()
        wait_all(results)

    @pl.when(plan[HELPS] == 0)
    def _():
        others = [
            copy(got1, rows.at[part(0, 6)], 4),
            copy(got_a.at[part(0, 4)], rows.at[part(6, 4)], 5),
            copy(got_a.at[pl.ds(8 * piece, piece)], rows.at[pl.ds(23 * piece, piece)], 6),
            copy(got_b.at[pl.ds(0, 3 * piece)], rows.at[pl.ds(20 * piece, 3 * piece)], 7),
            copy(got_b.at[pl.ds(3 * piece, 4 * piece)], rows.at[part(12, 2)], 8),
        ]
        start_all(others)
        out[0] = jnp.zeros_like(out[0])
        results = [pltpu.make_async_copy(out.at[0], gamma.at[1 - foreign], outs.at[0])]
        results[0].start()
        wait_all(others)
        pieces = ((6, 2, 2, 4), (4, 2, 0, 6), (2, 2, 8, 10), (1, 1, 12, 13))
        for n, (start, size, row0, row1) in enumerate(pieces):
            rows0 = rows[row0 * unit : (row0 + size) * unit]
            rows1 = rows[row1 * unit : (row1 + size) * unit]
            total = right(rows0, amp0[...]) + right(rows1, amp1[...])
            out[1, start * unit : (start + size) * unit] = total.astype(out.dtype)
            place = part(start, size)
            results.append(
                pltpu.make_async_copy(out.at[1, place], gamma.at[foreign, place], outs.at[1 + n])
            )
            results[-1].start()
        wait_all(results)


def put_kernel(unit, plan, back, gamma_in, gamma, sem):
    @pl.when(plan[HELPS] == 0)
    def _():
        copy = pltpu.make_async_copy(back, gamma.at[plan[FOREIGN], pl.ds(0, unit)], sem)
        copy.start()
        copy.wait()


def two_groups(factors, occ_energy, virt_energy, tile_table):
    owned, rows, width = factors.shape
    aux = lax.axis_size("aux")
    bits = aux.bit_length() - 1
    step, unit = rows // 4, rows // 8
    shard = width // aux
    dtype = factors.dtype
    dma = pltpu.SemaphoreType.DMA

    def array(*shape, dtype=dtype):
        return jax.ShapeDtypeStruct(shape, dtype)

    def call(kernel, out_shape, in_specs, out_specs, scratch, cost=0, mebi=16, **options):
        return pl.pallas_call(
            kernel,
            out_shape=out_shape,
            in_specs=in_specs,
            out_specs=out_specs,
            scratch_shapes=scratch,
            compiler_params=pltpu.CompilerParams(vmem_limit_bytes=mebi * MEBI),
            cost_estimate=pl.CostEstimate(
                flops=cost * 2 * step * width * width,
                bytes_accessed=2 * step * width * 2,
                transcendentals=0,
            ),
            **options,
        )

    plan, pay1 = call(
        functools.partial(plan_kernel, tile_table.shape[0], bits, step),
        (array(8, dtype=jnp.int32), array(3 * step, width)),
        [SMEM_SPEC, HBM_SPEC],
        (SMEM_SPEC, HBM_SPEC),
        [pltpu.VMEM((3 * step, width), dtype), dma((3, 2))],
        mebi=61,
    )(tile_table, factors)
    got1 = swap(pay1, "orb", 0)

    def halves(pairs):
        kept = array(pairs, width // 2, width, dtype=jnp.float32)
        return kept, array(pairs, width // 2, width, dtype=WIRE)

    square = pltpu.VMEM((width, width), jnp.float32)

    def scatter(kept, sent):
        upper = aux // 4

        def join(kept, came, shift, count):
            shape = (kept.shape[0], kept.shape[1] // count, width)
            return call(
                functools.partial(join_kernel, shift),
                (array(*shape, dtype=jnp.float32), *[array(*shape, dtype=WIRE)] * (count - 1)),
                [SMEM_SPEC, VMEM_SPEC, VMEM_SPEC],
                (VMEM_SPEC,) * count,
                [],
            )(plan, kept, came)

        kept, sent = join(kept, swap(sent, "aux", 0), bits - 2, 2)
        own, *sends = join(kept, direct(sent, bits, upper), 0, upper)
        for term in [direct(send, bits, 1 + n) for n, send in enumerate(sends)]:
            own = own + term.astype(jnp.float32)
        return own

    def prepare():
        return call(
            functools.partial(weigh_kernel, step),
            (
                array(1, shard, width, dtype=jnp.float32),
                array(2, shard, width, dtype=jnp.float32),
                array(9 * step // 4, width),
                array(7 * step // 4, width),
            ),
            [SMEM_SPEC, SMEM_SPEC, VMEM_SPEC, HBM_SPEC],
            (VMEM_SPEC, VMEM_SPEC, HBM_SPEC, HBM_SPEC),
            [pltpu.VMEM((4 * step, width), dtype), dma((6, 2))],
        )(plan, occ_energy, virt_energy, factors)

    def own_chain():
        kept, sent = call(
            functools.partial(own_kernel, step),
            halves(1),
            [SMEM_SPEC, HBM_SPEC],
            (VMEM_SPEC, VMEM_SPEC),
            [pltpu.VMEM(factors.shape, dtype), square, dma((4,))],
            4,
        )(plan, factors)
        own_weight, weights, pay_a, pay_b = prepare()
        shards01 = (scatter(kept, sent) * own_weight).astype(dtype)
        return gather_lower(shards01, bits), weights, pay_a, pay_b

    def no_chain():
        return jnp.zeros((aux // 4, 1, shard, width), dtype), *prepare()[1:]

    part01, weights, pay_a, pay_b = lax.cond(plan[COUNTS] > 0, own_chain, no_chain)
    used = plan[COUNTS + 1] + plan[COUNTS + 2] > 0
    got1, part01, weights, pay_a, used = lax.optimization_barrier(
        (got1, part01, weights, pay_a, used)
    )
    got_a = swap(pay_a, "orb", 0)

    def pair_chain():
        kept, sent = call(
            functools.partial(pair_kernel, step),
            halves(2),
            [SMEM_SPEC, HBM_SPEC, HBM_SPEC],
            (VMEM_SPEC, VMEM_SPEC),
            [
                pltpu.VMEM((3 * step, width), dtype),
                pltpu.VMEM((2 * step, width), dtype),
                pltpu.VMEM((3 * step, width), dtype),
                square,
                square,
                dma((8,)),
            ],
            5,
        )(plan, factors, got1)
        return scatter(kept, sent), *gather(part01, bits)

    def no_pairs():
        return jnp.zeros((2, shard, width), jnp.float32), *gather(part01, bits)

    sums, near01, far01 = lax.cond(used, pair_chain, no_pairs)
    sums, got_a, pay_b = lax.optimization_barrier((sums, got_a, pay_b))
    sums = sums + swap(sums.astype(WIRE), "orb", 0).astype(jnp.float32)
    shards0, pay_b = lax.optimization_barrier(((sums * weights).astype(dtype), pay_b))
    got_b = swap(pay_b, "orb", 0)

    amp = array(width, width)

    def amplitudes():
        near, far = gather(gather_lower(shards0, bits), bits)
        return call(
            back_kernel,
            (array(unit, width), amp, amp),
            [SMEM_SPEC, VMEM_SPEC, VMEM_SPEC, HBM_SPEC],
            (VMEM_SPEC,) * 3,
            [pltpu.VMEM((2, unit, width), dtype), dma],
            1,
        )(plan, near, far, factors)

    def nothing():
        zeros = jnp.zeros((width, width), dtype)
        return jnp.zeros((unit, width), dtype), zeros, zeros

    back, amp0, amp1 = lax.cond(used, amplitudes, nothing)
    got_back = swap(back, "orb", 0)

    gamma = call(
        functools.partial(last_kernel, step),
        array(*factors.shape),
        [SMEM_SPEC] + [HBM_SPEC] * 2 + [VMEM_SPEC] * 2 + [HBM_SPEC] * 4,
        HBM_SPEC,
        [
            pltpu.VMEM((2, *near01.shape), dtype),
            pltpu.VMEM((14 * unit, width), dtype),
            pltpu.VMEM(factors.shape, dtype),
            pltpu.VMEM(factors.shape, dtype),
            pltpu.VMEM((width, width), dtype),
            dma((12,)),
            dma((5,)),
        ],
        12,
        mebi=32,
    )(plan, near01, far01, amp0, amp1, got1, got_a, got_b, factors)
    return call(
        functools.partial(put_kernel, unit),
        array(*factors.shape),
        [SMEM_SPEC, VMEM_SPEC, HBM_SPEC],
        HBM_SPEC,
        [dma],
        input_output_aliases={2: 0},
    )(plan, got_back, gamma)


def shards(factors, occ_energy, virt_energy, tile_table):
    groups = lax.axis_size("orb")
    aux = lax.axis_size("aux")
    simple = groups == 2 and factors.shape[0] == 2 and tile_table.shape[0] <= CAP
    width = factors.shape[2]
    whole_shards = aux >= 4 and aux & (aux - 1) == 0 and width % (32 * aux) == 0
    if simple and whole_shards and factors.shape[1] % 256 == 0:
        return two_groups(factors, occ_energy, virt_energy, tile_table)
    return general(factors, occ_energy, virt_energy, tile_table)


def solution(mesh):
    return jax.shard_map(
        shards,
        mesh=mesh,
        in_specs=(P("orb", "aux", None), P(), P(), P()),
        out_specs=P("orb", "aux", None),
        check_vma=False,
    )
```

```python
import functools

import jax
import jax.numpy as jnp
from jax import lax
from jax.experimental import pallas as pl
from jax.experimental.pallas import tpu as pltpu
from jax.sharding import PartitionSpec as P

CAP = 4
WIRE = jnp.bfloat16
HELPS, FOREIGN, PLACE, COUNTS, LOW, PARTNER = 0, 1, 2, 3, 6, 7
MEBI = 1024 * 1024
SMEM_SPEC = pl.BlockSpec(memory_space=pltpu.SMEM)
HBM_SPEC = pl.BlockSpec(memory_space=pltpu.HBM)
VMEM_SPEC = pl.BlockSpec(memory_space=pltpu.VMEM)


def general(factors, occ_energy, virt_energy, tile_table):
    owned = factors.shape[0]
    width = factors.shape[2]
    tiles = tile_table.shape[0]
    groups = lax.axis_size("orb")
    mine = lax.axis_index("orb")
    first = tile_table[:, 0]
    second = tile_table[:, 1]
    helper = tile_table[:, 2]
    block_ids = jnp.arange(owned * groups, dtype=jnp.int32)
    group_ids = jnp.arange(groups, dtype=jnp.int32)
    local_ids = jnp.arange(owned, dtype=jnp.int32)
    touched = (
        (first[:, None] == block_ids[None, :]) | (second[:, None] == block_ids[None, :])
    ).astype(jnp.int32)
    helped = (helper[:, None] == group_ids[None, :]).astype(jnp.int32)
    usage = jnp.sum(helped[:, :, None] * touched[:, None, :], axis=0) > 0
    usage = usage.reshape(groups, groups, owned).astype(jnp.int32)
    own_usage = jnp.take(usage, mine, axis=1)
    send_pick = jnp.sum(own_usage * local_ids[None, :], axis=1)
    outgoing = jnp.stack(
        [
            lax.dynamic_index_in_dim(factors, send_pick[group], 0, keepdims=False)
            for group in range(groups)
        ]
    )
    incoming = lax.all_to_all(outgoing, "orb", split_axis=0, concat_axis=0, tiled=True)
    store = jnp.concatenate([factors, incoming], axis=0)

    def position(block):
        owner = block // owned
        return jnp.where(owner == mine, block % owned, owned + owner)

    is_mine = (helper == mine).astype(jnp.int32)
    tile_ids = jnp.arange(tiles, dtype=jnp.int32)
    earlier = (tile_ids[None, :] < tile_ids[:, None]).astype(jnp.int32)
    rank = jnp.sum(earlier * is_mine[None, :], axis=1)
    slot_ids = jnp.arange(CAP, dtype=jnp.int32)
    picked = is_mine[None, :] * (rank[None, :] == slot_ids[:, None]).astype(jnp.int32)
    valid = jnp.sum(picked, axis=1)
    tile_p = jnp.sum(picked * first[None, :], axis=1)
    tile_q = jnp.sum(picked * second[None, :], axis=1)
    place_p = position(tile_p)
    place_q = position(tile_q)
    energy_p = jnp.take(virt_energy, tile_p, axis=0)
    energy_q = jnp.take(virt_energy, tile_q, axis=0)
    occ_sum = jnp.take(occ_energy, tile_p) + jnp.take(occ_energy, tile_q)
    denominators = energy_p[:, :, None] + energy_q[:, None, :] - occ_sum[:, None, None]

    def partners(slot):
        block_p = lax.dynamic_index_in_dim(store, place_p[slot], 0, keepdims=False)
        block_q = lax.dynamic_index_in_dim(store, place_q[slot], 0, keepdims=False)
        return (block_p, block_q)

    def fill(slot, buffer):
        block_p, block_q = partners(slot)
        return lax.dynamic_update_index_in_dim(buffer, outer(block_p, block_q), slot, 0)

    buffer = lax.fori_loop(0, CAP, fill, jnp.zeros((CAP, width, width), jnp.float32))
    summed = lax.psum(buffer, "aux")
    all_amps = (summed / denominators).astype(jnp.bfloat16)

    def apply_all(slot, gathered):
        block_p, block_q = partners(slot)
        amplitudes = lax.dynamic_index_in_dim(all_amps, slot, 0, keepdims=False)
        amplitudes = jnp.where(valid[slot] > 0, amplitudes, jnp.zeros_like(amplitudes))
        gathered = gathered.at[place_p[slot]].add(right_t(block_q, amplitudes))
        return gathered.at[place_q[slot]].add(right(block_p, amplitudes))

    gathered = lax.fori_loop(0, CAP, apply_all, jnp.zeros(store.shape, jnp.float32))
    helper_part = gathered[owned:].astype(jnp.bfloat16)
    returned = lax.all_to_all(helper_part, "orb", split_axis=0, concat_axis=0, tiled=True)
    landing = (send_pick[:, None] == local_ids[None, :]).astype(jnp.float32)
    gamma = gathered[:owned] + jnp.einsum(
        "dj,dav->jav", landing, returned.astype(jnp.float32), precision=lax.Precision.HIGHEST
    )
    return gamma.astype(jnp.bfloat16)


def outer(a, b):
    return lax.dot_general(a, b, (((0,), (0,)), ((), ())), preferred_element_type=jnp.float32)


def right(a, m):
    return jnp.dot(a, m, preferred_element_type=jnp.float32)


def right_t(a, m):
    return lax.dot_general(a, m, (((1,), (1,)), ((), ())), preferred_element_type=jnp.float32)


def swap(value, axis, bit):
    size = lax.axis_size(axis)
    return lax.ppermute(value, axis, [(i, i ^ (1 << bit)) for i in range(size)])


def direct(value, bits, e):
    mask = sum(1 << (bits - 1 - n) for n in range(bits - 1) if (e >> n) & 1)
    size = 1 << bits
    return lax.ppermute(value, "aux", [(i, i ^ mask) for i in range(size)])


def gather(part, bits):
    near = jnp.concatenate([part, direct(part, bits, 1 << (bits - 2))], axis=0)
    return near, swap(near, "aux", 0)


def gather_lower(part, bits):
    upper = 1 << (bits - 2)
    pieces = [part[None]] + [direct(part, bits, e)[None] for e in range(1, upper)]
    while len(pieces) > 1:
        pieces = [jnp.concatenate(pieces[n : n + 2], axis=0) for n in range(0, len(pieces), 2)]
    return pieces[0]


def join_kernel(shift, plan, kept, came, own, *others):
    _, size, _ = own.shape
    count = 1 + len(others)
    place = (plan[PLACE] >> shift) & (count - 1)
    for e, out in enumerate((own, *others)):
        rows = pl.ds(pl.multiple_of((place ^ e) * size, size), size)
        total = kept[:, rows, :] + came[:, rows, :].astype(jnp.float32)
        out[...] = total.astype(out.dtype)


def after(value, *others):
    return lax.optimization_barrier((value, *others))[0]


def start_all(copies):
    for copy in copies:
        copy.start()


def wait_all(copies):
    for copy in copies:
        copy.wait()


def staged(source, stage, target, sems):
    first = pltpu.make_async_copy(source, stage, sems.at[0])
    return first, pltpu.make_async_copy(stage, target, sems.at[1])


def relay(copies):
    for first, second in copies:
        first.wait()
        second.start()


def rows_at(unit, start, size):
    return pl.ds(pl.multiple_of(start * unit, unit), size * unit)


def plan_kernel(tiles, bits, step, table, factors, plan, pay, stage, sems):
    helper = table[0, 2]
    helps = (lax.axis_index("orb") == helper).astype(jnp.int32)
    low, foreign_low = helper * 2, (1 - helper) * 2
    foreign = jnp.int32(0)
    for t in range(tiles):
        named = (table[t, 0] == foreign_low + 1) | (table[t, 1] == foreign_low + 1)
        foreign = foreign | named.astype(jnp.int32)
    b0, b1 = jnp.where(helps == 1, 0, foreign), jnp.where(helps == 1, 1, foreign)
    sources = ((b0, 2 * helps), (b0, 2 * helps + 1), (b1, 2 + helps))
    copies = [
        staged(
            factors.at[block, rows_at(step, start, 1)],
            stage.at[pl.ds(n * step, step)],
            pay.at[pl.ds(n * step, step)],
            sems.at[n],
        )
        for n, (block, start) in enumerate(sources)
    ]
    start_all(first for first, _ in copies)
    me = lax.axis_index("aux")
    place = jnp.int32(0)
    for bit in range(bits):
        place = place * 2 + ((me >> bit) & 1)
    plan[HELPS], plan[FOREIGN], plan[PLACE] = helps, foreign, place
    plan[LOW], plan[PARTNER] = low, foreign_low + foreign
    pairs = ((low, low + 1), (low, foreign_low + foreign), (low + 1, foreign_low + foreign))
    for n, (a, b) in enumerate(pairs):
        count = jnp.int32(0)
        for t in range(tiles):
            p, q = table[t, 0], table[t, 1]
            same = ((p == a) & (q == b)) | ((p == b) & (q == a))
            count = count + same.astype(jnp.int32)
        plan[COUNTS + n] = count
    relay(copies)
    wait_all(second for _, second in copies)


def weigh_kernel(step, plan, occ, virt, factors, own_weight, weights, pay_a, pay_b, stage, sems):
    piece = step // 4
    helps, foreign = plan[HELPS], plan[FOREIGN]
    b0, b1 = jnp.where(helps == 1, 0, foreign), jnp.where(helps == 1, 1, foreign)
    moves = (
        (b1, 12 - 4 * helps, 4, pay_a, 0, 0),
        (b0, 4, 4, pay_a, 4, 4),
        (b1, 7, 1, pay_a, 8, 8),
        (b1, 4, 3, pay_b, 0, 9),
        (b0, 2, 2, pay_b, 3, 12),
        (b1, 2, 2, pay_b, 5, 14),
    )
    copies = [
        staged(
            factors.at[block, rows_at(piece, start, size)],
            stage.at[pl.ds(between * piece, size * piece)],
            pay.at[pl.ds(to * piece, size * piece)],
            sems.at[n],
        )
        for n, (block, start, size, pay, to, between) in enumerate(moves)
    ]
    start_all(first for first, _ in copies)
    low, partner = plan[LOW], plan[PARTNER]
    _, shard, width = own_weight.shape
    row = lax.broadcasted_iota(jnp.int32, (shard, width), 0)
    column = lax.broadcasted_iota(jnp.int32, (shard, width), 1)
    mine = column == row + plan[PLACE] * shard
    pairs = ((low, low + 1, own_weight, 0), (low, partner, weights, 0), (low + 1, partner, weights, 1))
    for n, (a, b, out, slot) in enumerate(pairs):
        virt_a = jnp.sum(jnp.where(mine, virt[pl.ds(a, 1), :], 0.0), axis=1, keepdims=True)
        denominators = virt_a + virt[pl.ds(b, 1), :] - occ[a] - occ[b]
        out[slot] = plan[COUNTS + n].astype(jnp.float32) / denominators
    relay(copies)
    wait_all(second for _, second in copies)


def split_halves(acc, pair, kept, sent, core):
    half = kept.shape[1]
    kept[pair] = acc[pl.ds(pl.multiple_of(core * half, half), half), :]
    other = acc[pl.ds(pl.multiple_of((1 - core) * half, half), half), :]
    sent[pair] = other.astype(sent.dtype)


def own_kernel(step, plan, factors, kept, sent, rows, acc, sems):
    del plan
    copies = [
        pltpu.make_async_copy(
            factors.at[:, pl.ds(n * step, step)], rows.at[:, pl.ds(n * step, step)], sems.at[n]
        )
        for n in range(4)
    ]
    start_all(copies)
    for n in range(4):
        copies[n].wait()
        term = outer(rows[0, n * step : (n + 1) * step], rows[1, n * step : (n + 1) * step])
        acc[...] = term if n == 0 else acc[...] + term
    split_halves(acc, 0, kept, sent, lax.axis_index("aux") & 1)


def pair_kernel(
    step, plan, factors, got_hbm, kept, sent, got, rows0, rows1, acc0, acc1, sems
):
    helps, foreign = plan[HELPS], plan[FOREIGN]
    b0, b1 = jnp.where(helps == 1, 0, foreign), jnp.where(helps == 1, 1, foreign)

    def cut(ref, n):
        return ref[n * step : (n + 1) * step]

    def fetch(source, ref, n, slot):
        return pltpu.make_async_copy(source, ref.at[pl.ds(n * step, step)], sems.at[slot])

    gots = [fetch(got_hbm.at[pl.ds(n * step, step)], got, n, n) for n in range(3)]
    copies0 = [
        fetch(factors.at[b0, rows_at(step, jnp.where(helps == 1, n, 2 + n), 1)], rows0, n, 3 + n)
        for n in range(2)
    ]
    copies1 = [
        fetch(factors.at[b1, rows_at(step, jnp.where(helps == 1, n, 3), 1)], rows1, n, 5 + n)
        for n in range(3)
    ]
    start_all((gots[0], copies0[0], gots[1], copies0[1], gots[2], copies1[2], *copies1[:2]))

    for n in range(2):
        wait_all((gots[n], copies0[n]))

        @pl.when(helps == 1)
        def _():
            term = outer(cut(rows0, n), cut(got, n))
            acc0[...] = term if n == 0 else acc0[...] + term

        @pl.when(helps == 0)
        def _():
            term = outer(cut(got, n), cut(rows0, n))
            acc0[...] = term if n == 0 else acc0[...] + term

    wait_all((gots[2], copies1[2]))

    @pl.when(helps == 1)
    def _():
        acc1[...] = outer(cut(rows1, 2), cut(got, 2))

    @pl.when(helps == 0)
    def _():
        acc1[...] = outer(cut(got, 2), cut(rows1, 2))

    wait_all(copies1[:2])

    @pl.when(helps == 1)
    def _():
        acc1[...] += outer(cut(rows1, 0), cut(got, 0)) + outer(cut(rows1, 1), cut(got, 1))

    core = lax.axis_index("aux") & 1
    split_halves(acc0, 0, kept, sent, core)
    split_halves(acc1, 1, kept, sent, core)


def arrange(plan, near, far, pair, out):
    count, _, shard, _ = near.shape
    for source, base in ((near, 0), (far, count)):
        for n in range(count):
            row = pl.multiple_of((plan[PLACE] ^ (base + n)) * shard, shard)
            out[pl.ds(row, shard), :] = source[n, pair]


def back_kernel(plan, near, far, factors, back, amp0, amp1, rows, sem):
    copy = pltpu.make_async_copy(factors.at[:, pl.ds(0, back.shape[0])], rows, sem)
    copy.start()
    arrange(plan, near, far, 0, amp0)
    arrange(plan, near, far, 1, amp1)
    copy.wait()
    total = right(rows[0], amp0[...]) + right(rows[1], amp1[...])
    back[...] = total.astype(back.dtype)


def last_kernel(
    step, plan, near01, far01, amp0, amp1, got1, got_a, got_b, factors, gamma, small, rows, own, out, own_amp, ins, outs
):
    unit, piece = step // 2, step // 4
    foreign = plan[FOREIGN]

    def part(start, size):
        return pl.ds(start * unit, size * unit)

    def copy(source, target, slot):
        return pltpu.make_async_copy(source, target, ins.at[slot])

    @pl.when(plan[HELPS] == 1)
    def _():
        singles = [copy(near01, small.at[0], 2), copy(far01, small.at[1], 3)]
        sources = [got1.at[part(2 * n, 2)] for n in range(3)] + [got_a.at[part(0, 2)]]
        others = [copy(sources[n], rows.at[part(2 * n, 2)], 4 + n) for n in range(4)]
        mine = [copy(factors.at[:, part(2 * n, 2)], own.at[:, part(2 * n, 2)], 8 + n) for n in range(4)]
        start_all(singles)
        for n in range(4):
            start_all((mine[n], others[n]))
        wait_all(singles)
        arrange(plan, small.at[0], small.at[1], 0, own_amp)
        results = []
        for n in range(4):
            wait_all((mine[n], others[n]))
            at = slice(n * step, (n + 1) * step)
            first = right_t(own[1, at], own_amp[...]) + right_t(rows[at], amp0[...])
            out[0, at] = first.astype(out.dtype)
            place = part(2 * n, 2)
            results.append(pltpu.make_async_copy(out.at[0, place], gamma.at[0, place], outs.at[n]))
            results[-1].start()
            second = right(own[0, at], own_amp[...]) + right_t(rows[at], amp1[...])
            out[1, at] = second.astype(out.dtype)
            results.append(
                pltpu.make_async_copy(out.at[1, place], gamma.at[1, place], outs.at[4 + n])
            )
            results[-1].start()
        wait_all(results)

    @pl.when(plan[HELPS] == 0)
    def _():
        others = [
            copy(got1, rows.at[part(0, 6)], 4),
            copy(got_a.at[part(0, 4)], rows.at[part(6, 4)], 5),
            copy(got_a.at[pl.ds(8 * piece, piece)], rows.at[pl.ds(23 * piece, piece)], 6),
            copy(got_b.at[pl.ds(0, 3 * piece)], rows.at[pl.ds(20 * piece, 3 * piece)], 7),
            copy(got_b.at[pl.ds(3 * piece, 4 * piece)], rows.at[part(12, 2)], 8),
        ]
        start_all(others)
        out[0] = jnp.zeros_like(out[0])
        results = [pltpu.make_async_copy(out.at[0], gamma.at[1 - foreign], outs.at[0])]
        results[0].start()
        wait_all(others)
        pieces = ((6, 2, 2, 4), (4, 2, 0, 6), (2, 2, 8, 10), (1, 1, 12, 13))
        for n, (start, size, row0, row1) in enumerate(pieces):
            rows0 = rows[row0 * unit : (row0 + size) * unit]
            rows1 = rows[row1 * unit : (row1 + size) * unit]
            total = right(rows0, amp0[...]) + right(rows1, amp1[...])
            out[1, start * unit : (start + size) * unit] = total.astype(out.dtype)
            place = part(start, size)
            results.append(
                pltpu.make_async_copy(out.at[1, place], gamma.at[foreign, place], outs.at[1 + n])
            )
            results[-1].start()
        wait_all(results)


def put_kernel(unit, plan, back, gamma_in, gamma, sem):
    @pl.when(plan[HELPS] == 0)
    def _():
        copy = pltpu.make_async_copy(back, gamma.at[plan[FOREIGN], pl.ds(0, unit)], sem)
        copy.start()
        copy.wait()


def two_groups(factors, occ_energy, virt_energy, tile_table):
    owned, rows, width = factors.shape
    aux = lax.axis_size("aux")
    bits = aux.bit_length() - 1
    step, unit = rows // 4, rows // 8
    shard = width // aux
    dtype = factors.dtype
    dma = pltpu.SemaphoreType.DMA

    def array(*shape, dtype=dtype):
        return jax.ShapeDtypeStruct(shape, dtype)

    def call(kernel, out_shape, in_specs, out_specs, scratch, cost=0, mebi=16, **options):
        return pl.pallas_call(
            kernel,
            out_shape=out_shape,
            in_specs=in_specs,
            out_specs=out_specs,
            scratch_shapes=scratch,
            compiler_params=pltpu.CompilerParams(vmem_limit_bytes=mebi * MEBI),
            cost_estimate=pl.CostEstimate(
                flops=cost * 2 * step * width * width,
                bytes_accessed=2 * step * width * 2,
                transcendentals=0,
            ),
            **options,
        )

    plan, pay1 = call(
        functools.partial(plan_kernel, tile_table.shape[0], bits, step),
        (array(8, dtype=jnp.int32), array(3 * step, width)),
        [SMEM_SPEC, HBM_SPEC],
        (SMEM_SPEC, HBM_SPEC),
        [pltpu.VMEM((3 * step, width), dtype), dma((3, 2))],
        mebi=61,
    )(tile_table, factors)
    got1 = swap(pay1, "orb", 0)

    def halves(pairs):
        kept = array(pairs, width // 2, width, dtype=jnp.float32)
        return kept, array(pairs, width // 2, width, dtype=WIRE)

    square = pltpu.VMEM((width, width), jnp.float32)

    def scatter(kept, sent):
        upper = aux // 4

        def join(kept, came, shift, count):
            shape = (kept.shape[0], kept.shape[1] // count, width)
            return call(
                functools.partial(join_kernel, shift),
                (array(*shape, dtype=jnp.float32), *[array(*shape, dtype=WIRE)] * (count - 1)),
                [SMEM_SPEC, VMEM_SPEC, VMEM_SPEC],
                (VMEM_SPEC,) * count,
                [],
            )(plan, kept, came)

        kept, sent = join(kept, swap(sent, "aux", 0), bits - 2, 2)
        own, *sends = join(kept, direct(sent, bits, upper), 0, upper)
        for term in [direct(send, bits, 1 + n) for n, send in enumerate(sends)]:
            own = own + term.astype(jnp.float32)
        return own

    def prepare():
        return call(
            functools.partial(weigh_kernel, step),
            (
                array(1, shard, width, dtype=jnp.float32),
                array(2, shard, width, dtype=jnp.float32),
                array(9 * step // 4, width),
                array(7 * step // 4, width),
            ),
            [SMEM_SPEC, SMEM_SPEC, VMEM_SPEC, HBM_SPEC],
            (VMEM_SPEC, VMEM_SPEC, HBM_SPEC, HBM_SPEC),
            [pltpu.VMEM((4 * step, width), dtype), dma((6, 2))],
        )(plan, occ_energy, virt_energy, factors)

    def own_chain():
        kept, sent = call(
            functools.partial(own_kernel, step),
            halves(1),
            [SMEM_SPEC, HBM_SPEC],
            (VMEM_SPEC, VMEM_SPEC),
            [pltpu.VMEM(factors.shape, dtype), square, dma((4,))],
            4,
        )(plan, factors)
        own_weight, weights, pay_a, pay_b = prepare()
        shards01 = (scatter(kept, sent) * own_weight).astype(dtype)
        return gather_lower(shards01, bits), weights, pay_a, pay_b

    def no_chain():
        return jnp.zeros((aux // 4, 1, shard, width), dtype), *prepare()[1:]

    part01, weights, pay_a, pay_b = lax.cond(plan[COUNTS] > 0, own_chain, no_chain)
    used = plan[COUNTS + 1] + plan[COUNTS + 2] > 0
    got1, part01, weights, pay_a, used = lax.optimization_barrier(
        (got1, part01, weights, pay_a, used)
    )
    got_a = swap(pay_a, "orb", 0)

    def pair_chain():
        kept, sent = call(
            functools.partial(pair_kernel, step),
            halves(2),
            [SMEM_SPEC, HBM_SPEC, HBM_SPEC],
            (VMEM_SPEC, VMEM_SPEC),
            [
                pltpu.VMEM((3 * step, width), dtype),
                pltpu.VMEM((2 * step, width), dtype),
                pltpu.VMEM((3 * step, width), dtype),
                square,
                square,
                dma((8,)),
            ],
            5,
        )(plan, factors, got1)
        return scatter(kept, sent), *gather(part01, bits)

    def no_pairs():
        return jnp.zeros((2, shard, width), jnp.float32), *gather(part01, bits)

    sums, near01, far01 = lax.cond(used, pair_chain, no_pairs)
    sums, got_a, pay_b = lax.optimization_barrier((sums, got_a, pay_b))
    sums = sums + swap(sums.astype(WIRE), "orb", 0).astype(jnp.float32)
    shards0, pay_b = lax.optimization_barrier(((sums * weights).astype(dtype), pay_b))
    got_b = swap(pay_b, "orb", 0)

    amp = array(width, width)

    def amplitudes():
        near, far = gather(gather_lower(shards0, bits), bits)
        return call(
            back_kernel,
            (array(unit, width), amp, amp),
            [SMEM_SPEC, VMEM_SPEC, VMEM_SPEC, HBM_SPEC],
            (VMEM_SPEC,) * 3,
            [pltpu.VMEM((2, unit, width), dtype), dma],
            1,
        )(plan, near, far, factors)

    def nothing():
        zeros = jnp.zeros((width, width), dtype)
        return jnp.zeros((unit, width), dtype), zeros, zeros

    back, amp0, amp1 = lax.cond(used, amplitudes, nothing)
    got_back = swap(back, "orb", 0)

    gamma = call(
        functools.partial(last_kernel, step),
        array(*factors.shape),
        [SMEM_SPEC] + [HBM_SPEC] * 2 + [VMEM_SPEC] * 2 + [HBM_SPEC] * 4,
        HBM_SPEC,
        [
            pltpu.VMEM((2, *near01.shape), dtype),
            pltpu.VMEM((14 * unit, width), dtype),
            pltpu.VMEM(factors.shape, dtype),
            pltpu.VMEM(factors.shape, dtype),
            pltpu.VMEM((width, width), dtype),
            dma((12,)),
            dma((8,)),
        ],
        12,
        mebi=32,
    )(plan, near01, far01, amp0, amp1, got1, got_a, got_b, factors)
    return call(
        functools.partial(put_kernel, unit),
        array(*factors.shape),
        [SMEM_SPEC, VMEM_SPEC, HBM_SPEC],
        HBM_SPEC,
        [dma],
        input_output_aliases={2: 0},
    )(plan, got_back, gamma)


def shards(factors, occ_energy, virt_energy, tile_table):
    groups = lax.axis_size("orb")
    aux = lax.axis_size("aux")
    simple = groups == 2 and factors.shape[0] == 2 and tile_table.shape[0] <= CAP
    width = factors.shape[2]
    whole_shards = aux >= 4 and aux & (aux - 1) == 0 and width % (32 * aux) == 0
    if simple and whole_shards and factors.shape[1] % 256 == 0:
        return two_groups(factors, occ_energy, virt_energy, tile_table)
    return general(factors, occ_energy, virt_energy, tile_table)


def solution(mesh):
    return jax.shard_map(
        shards,
        mesh=mesh,
        in_specs=(P("orb", "aux", None), P(), P(), P()),
        out_specs=P("orb", "aux", None),
        check_vma=False,
    )
```
